512 devices in a mesh: batch: 128 (over z, x_hi, y), dp: 4 (over x_lo, core).
Axes of the slice: x: 4 (x_hi: 2, x_lo: 2; x = x_hi * 2 + x_lo), y: 4, z: 16, core: 2. Of those that a mesh axis runs over, the one named last changes fastest.
Arguments:
- query_states: bfloat16 [4, 16384, 1024], P('dp', 'batch')
- passage_states: bfloat16 [4, 16384, 1024], P('dp', 'batch')
- loss_weights: float32 [4, 16384], P('dp', 'batch'), may hold values from 0.25 to 4
- positives: int32 [4, 16384], P('dp', 'batch'), may hold values from 0 to 16383, as said below
- head_weight: bfloat16 [1024, 1024], replicated, may hold values from -0.1875 to 0.1875
Outputs:
- query_grad: bfloat16 [4, 16384, 1024], P('dp', 'batch')
- passage_grad: bfloat16 [4, 16384, 1024], P('dp', 'batch')
- head_grad: float32 [1024, 1024], P(('batch', 'dp'))
The draws below stay inside these ranges and needn't reach their ends.
Inputs may be any that keep to these rules, and one draw needn't show every extreme that they name: Each block of 128 rows pairs its queries one to one with its own passages: the positives of block b are a permutation of b * 128 to b * 128 + 127.
All inputs are finite; a program needn't handle non-finite values.
Results may differ from the reference program's by a relative error of at most 0.0095.
Values may be sent and summed in bfloat16 or wider, within the bound.
No kernel may reach another device: no remote copies, remote signals or barrier semaphores. Data moves between devices by JAX's collectives and lax.ppermute only.
A program may use at most 64 MiB of HBM per device.

```python
import math
import jax
import jax.numpy as jnp
from jax import lax

HID = 1024
D = 1024
ROWS = 128
BATCH = 16384
N_DP = 4


def passage_base(key):
    return jax.random.normal(key, (N_DP, BATCH, HID), jnp.float32)


def draw_passage_states(key, part):
    base = passage_base(key)
    return jnp.clip(base, -6.0, 6.0).astype(jnp.bfloat16)


def draw_query_states(key, part):
    key = jax.random.fold_in(key, 13)
    queries = jax.random.normal(key, (N_DP, BATCH, HID), jnp.float32)
    return jnp.clip(queries, -6.0, 6.0).astype(jnp.bfloat16)


def draw_positives(key, part):
    key = jax.random.fold_in(key, 17)
    count = N_DP * (BATCH // ROWS)
    keys = jax.random.split(key, count)
    perms = jax.vmap(lambda k: jax.random.permutation(k, ROWS))(keys).astype(jnp.int32)
    offsets = jnp.arange(count, dtype=jnp.int32) % (BATCH // ROWS) * ROWS
    return (perms + offsets[:, None]).reshape(N_DP, BATCH).astype(jnp.int32)


def level_of(own_key, dims, pieces, low, high):
    def one(axis_at, blocks):
        steps = jax.random.uniform(jax.random.fold_in(jax.random.fold_in(own_key, 6), axis_at), (blocks,), jnp.float32, low / len(pieces), high / len(pieces))
        return jnp.repeat(jnp.exp(steps), dims[axis_at] // blocks).reshape((-1,) + (1,) * (len(dims) - axis_at - 1))

    gain = one(*pieces[0])
    for cut in pieces[1:]:
        gain = gain * one(*cut)
    return gain


def centred(rng, extent, width, bound, kind=jnp.bfloat16):
    result = width * jax.random.normal(rng, extent, jnp.float32)
    return jnp.clip(result, min=-bound, max=bound).astype(kind)


def setup_inputs(seed: int = 0) -> dict:
    arg_keys = jax.random.split(jax.random.key(seed), 6)
    return {
        "query_states": draw_query_states(jax.random.fold_in(arg_keys[5], 71), 0),
        "passage_states": draw_passage_states(jax.random.fold_in(arg_keys[5], 71), 0),
        "loss_weights": jnp.clip(jnp.exp(math.log(4.0) - 2.7725887 * jax.random.uniform(arg_keys[2], (N_DP, BATCH), jnp.float32) ** level_of(arg_keys[2], (N_DP, BATCH), ((0, 4), (1, 128)), -0.2, 0.2)), 0.25, 4.0),
        "positives": draw_positives(jax.random.fold_in(arg_keys[5], 71), 0),
        "head_weight": centred(arg_keys[4], (HID, D), HID ** -0.5, 0.1875),
    }


score_scale = 0.1


def reference(query_states, passage_states, loss_weights, positives, head_weight):
    blocks_n = BATCH // ROWS

    def group(args):
        hq, hp, cw, pos = args
        eq = jnp.dot(hq, head_weight, preferred_element_type=jnp.float32).astype(jnp.bfloat16)
        ep = jnp.dot(hp, head_weight, preferred_element_type=jnp.float32).astype(jnp.bfloat16)
        eqb = eq.reshape(blocks_n, ROWS, D)
        epb = ep.reshape(blocks_n, ROWS, D)
        nearby = jnp.stack([jnp.roll(epb, k, axis=0) for k in range(3)], 1)
        cwb = cw.reshape(blocks_n, ROWS)
        posb = (pos % ROWS).reshape(blocks_n, ROWS)

        def one_block(items):
            query, near, weight, local = items
            flat = near.reshape(3 * ROWS, D)
            scores = jnp.dot(query, flat.T, preferred_element_type=jnp.float32) * score_scale
            top = jnp.max(scores, axis=1, keepdims=True)
            lse = top + jnp.log(jnp.sum(jnp.exp(scores - top), axis=1, keepdims=True))
            onehot = (jnp.arange(3 * ROWS, dtype=jnp.int32)[None, :] == local[:, None]).astype(jnp.float32)
            dscores = (weight[:, None] * score_scale * (jnp.exp(scores - lse) - onehot)).astype(jnp.bfloat16)
            gq = jnp.dot(dscores, flat, preferred_element_type=jnp.float32)
            parts = jnp.dot(dscores.T, query, preferred_element_type=jnp.float32)
            return gq, parts.reshape(3, ROWS, D)

        gq, parts = lax.map(one_block, (eqb, nearby, cwb, posb))
        gep = parts[:, 0]
        for k in range(1, 3):
            gep = gep + jnp.roll(parts[:, k], -k, axis=0)
        gq = gq.reshape(BATCH, D).astype(jnp.bfloat16)
        gep = gep.reshape(BATCH, D).astype(jnp.bfloat16)
        grad_q = jnp.dot(gq, head_weight.T, preferred_element_type=jnp.float32).astype(jnp.bfloat16)
        grad_p = jnp.dot(gep, head_weight.T, preferred_element_type=jnp.float32).astype(jnp.bfloat16)
        grad_w = jnp.dot(hq.T, gq, preferred_element_type=jnp.float32) + jnp.dot(hp.T, gep, preferred_element_type=jnp.float32)
        return grad_q, grad_p, grad_w

    grad_q, grad_p, grad_w = lax.map(group, (query_states, passage_states, loss_weights, positives))
    return grad_q, grad_p, jnp.sum(grad_w, axis=0)
```

```python
import jax
import jax.numpy as jnp
import numpy as np
from jax import lax
from jax.sharding import Mesh, PartitionSpec as P

ROWS = 128
AXES = ("z", "xh", "y", "xl", "c")
SIZES = (16, 2, 4, 2, 2)
BATCH = ("z", "xh", "y")
PLANE = ("xh", "y", "xl")
DP = ("xl", "c")

score_scale = 0.1


def shifted(block, distance):
    n = lax.axis_size(BATCH)
    return lax.ppermute(block, BATCH, [(i, (i + distance) % n) for i in range(n)])


def after(value, *others):
    return lax.optimization_barrier((value, *others))[0]


def mm(a, b):
    return jnp.dot(a, b, preferred_element_type=jnp.float32)


def nt(a, b):
    return lax.dot_general(a, b, (((1,), (1,)), ((), ())), preferred_element_type=jnp.float32)


def tn(a, b):
    return lax.dot_general(a, b, (((0,), (0,)), ((), ())), preferred_element_type=jnp.float32)


def row_of_position(core):
    pos = jnp.arange(1024, dtype=jnp.int32)
    half, plane, z, t = pos >> 9, (pos >> 5) & 15, (pos >> 1) & 15, pos & 1
    c = jnp.where(half == 0, 1 - core, core)
    return z * 64 + (plane >> 3) * 32 + ((plane >> 1) & 3) * 8 + (plane & 1) * 4 + c * 2 + t


def body(query_states, passage_states, loss_weights, positives, head_weight):
    hq = query_states[0]
    hp = passage_states[0]
    weight = loss_weights[0]
    local = positives[0] % ROWS
    bf16 = jnp.bfloat16

    hp1 = shifted(hp, 1)
    hp2 = shifted(hp, 2)

    eq = mm(hq, head_weight).astype(bf16)
    ep0 = mm(hp, head_weight).astype(bf16)
    rows = row_of_position(lax.axis_index("c"))
    pick = (jnp.arange(1024, dtype=jnp.int32)[:, None] == rows[None, :]).astype(bf16)
    own_h = mm(jnp.concatenate([hq, hp], axis=0), pick).astype(bf16)

    near = jnp.concatenate([hp1, hp2], axis=0)
    far_h = mm(near, pick).astype(bf16)
    ep12 = mm(near, head_weight).astype(bf16)
    ep = jnp.concatenate([ep0, ep12], axis=0)
    scores = nt(eq, ep) * score_scale
    top = jnp.max(scores, axis=1, keepdims=True)
    lse = top + jnp.log(jnp.sum(jnp.exp(scores - top), axis=1, keepdims=True))
    onehot = (jnp.arange(3 * ROWS, dtype=jnp.int32)[None, :] == local[:, None]).astype(jnp.float32)
    ds = (weight[:, None] * score_scale * (jnp.exp(scores - lse) - onehot)).astype(bf16)
    parts = tn(ds, eq)
    part0 = parts[:ROWS]
    part1 = parts[ROWS : 2 * ROWS]
    part2_low = parts[2 * ROWS :].astype(bf16)
    back2 = shifted(part2_low, -1)

    gq = mm(ds, ep).astype(bf16)
    states = jnp.concatenate([own_h, far_h], axis=0)
    grads = jnp.concatenate([gq, parts.astype(bf16)], axis=0)
    theirs = tn(states[:, :512], grads).astype(bf16)
    swapped = lax.ppermute(theirs, "c", [(0, 1), (1, 0)])
    mine = tn(states[:, 512:], grads)
    grad_q = nt(gq, head_weight).astype(bf16)
    chip = (mine + swapped).astype(bf16)

    pieces = lax.all_to_all(chip, PLANE, 0, 0, tiled=True)
    plane = jnp.sum(pieces.reshape(16, 32, 1024).astype(jnp.float32), axis=0)

    part1 = after(part1, plane)
    carried = (back2 + part1).astype(bf16)
    back1 = shifted(carried, -1)
    plane = after(plane, carried).reshape(16 * 16, 128)
    pieces = lax.all_to_all(plane, "z", 0, 0, tiled=True)
    head_grad = jnp.sum(pieces.reshape(16, 16, 128), axis=0).reshape(2, 1024)

    part0 = after(part0, head_grad)
    gep = (part0 + back1).astype(bf16)
    grad_p = nt(gep, head_weight).astype(bf16)
    return (grad_q[None], grad_p[None], head_grad)


def solution(mesh):
    fine = Mesh(mesh.devices.reshape(SIZES), AXES)
    in_specs = (P(DP, BATCH, None), P(DP, BATCH, None), P(DP, BATCH), P(DP, BATCH), P())
    out_specs = (P(DP, BATCH, None), P(DP, BATCH, None), P((*BATCH, *DP), None))
    return jax.shard_map(body, mesh=fine, in_specs=in_specs, out_specs=out_specs, check_vma=False)
```

```python
import jax
import jax.numpy as jnp
from jax import lax
from jax.experimental import pallas as pl
from jax.experimental.pallas import tpu as pltpu
from jax.sharding import Mesh, PartitionSpec as P

ROWS = 128
AXES = ("z", "xh", "y", "xl", "c")
SIZES = (16, 2, 4, 2, 2)
BATCH = ("z", "xh", "y")
CHIPS = ("z", "xh", "y", "xl")
PLANE = ("xh", "y", "xl")
DP = ("xl", "c")
WIDTH = 1024
HALF = WIDTH // 2

score_scale = 0.1
bf16 = jnp.bfloat16
f32 = jnp.float32


def shifted(block, distance):
    n = lax.axis_size(BATCH)
    return lax.ppermute(block, BATCH, [(i, (i + distance) % n) for i in range(n)])


def chip_index(x, y, z):
    x, y, z = x % 4, y % 4, z % 16
    return ((z * 2 + x // 2) * 4 + y) * 2 + x % 2


def chip_route(target):
    pairs = []
    for z in range(16):
        for y in range(4):
            for x in range(4):
                to = target(x, y, z)
                if to is not None:
                    pairs.append((chip_index(x, y, z), chip_index(*to)))
    return pairs


def step_back(x, y, z):
    return (x, y - 1, z) if y else (x - 1, 3, z)


def relay_back(x, y, z):
    return (x - 1, 2, z - (1 if (x + 1) % 4 < 2 else 0)) if y == 3 else None


def after(value, *others):
    return lax.optimization_barrier((value, *others))[0]


def mm(a, b):
    return jnp.dot(a, b, preferred_element_type=f32)


def nt(a, b):
    return lax.dot_general(a, b, (((1,), (1,)), ((), ())), preferred_element_type=f32)


def project_kernel(core_ref, hq_ref, hp_ref, w_ref, eq_ref, ep_ref, pick_ref, held_ref):
    eq_ref[...] = mm(hq_ref[...], w_ref[...]).astype(bf16)
    ep_ref[...] = mm(hp_ref[...], w_ref[...]).astype(bf16)
    core = core_ref[0]
    pos = lax.broadcasted_iota(jnp.int32, (WIDTH, 128), 0)
    lane = lax.broadcasted_iota(jnp.int32, (WIDTH, 128), 1)
    plane, z, t = (pos >> 5) & 15, (pos >> 1) & 15, pos & 1
    c = jnp.where(pos < HALF, 1 - core, core)
    row = z * 64 + (plane >> 3) * 32 + ((plane >> 1) & 3) * 8 + (plane & 1) * 4 + c * 2 + t
    for j in range(WIDTH // 128):
        pick_ref[:, j * 128 : (j + 1) * 128] = jnp.where(row == lane + j * 128, 1.0, 0.0).astype(bf16)
    held_ref[:, :ROWS] = nt(pick_ref[...], hq_ref[...]).astype(bf16)
    held_ref[:, ROWS:] = nt(pick_ref[...], hp_ref[...]).astype(bf16)


def first_kernel(hp_ref, w_ref, pick_ref, ep_ref, held_ref):
    ep_ref[...] = mm(hp_ref[...], w_ref[...]).astype(bf16)
    held_ref[...] = nt(pick_ref[...], hp_ref[...]).astype(bf16)


def grads_kernel(
    hp_ref, w_ref, pick_ref, eq_ref, ep0_ref, ep1_ref, held_ref, held1_ref, weight_ref, local_ref,
    part0_ref, part1_ref, part2_ref, g_ref, held2_ref, theirs_ref, ep_ref,
):
    ep_ref[:ROWS] = ep0_ref[...]
    ep_ref[ROWS : 2 * ROWS] = ep1_ref[...]
    ep_ref[2 * ROWS :] = mm(hp_ref[...], w_ref[...]).astype(bf16)
    held2_ref[...] = nt(pick_ref[...], hp_ref[...]).astype(bf16)
    scores = nt(eq_ref[...], ep_ref[...]) * score_scale
    top = jnp.max(scores, axis=1, keepdims=True)
    lse = top + jnp.log(jnp.sum(jnp.exp(scores - top), axis=1, keepdims=True))
    column = lax.broadcasted_iota(jnp.int32, (ROWS, 3 * ROWS), 1)
    onehot = jnp.where(column == local_ref[...], 1.0, 0.0)
    ds = (weight_ref[...] * score_scale * (jnp.exp(scores - lse) - onehot)).astype(bf16)
    g_ref[:ROWS] = mm(ds, ep_ref[...]).astype(bf16)
    parts = mm(ds.astype(f32).T.astype(bf16), eq_ref[...])
    part0_ref[...] = parts[:ROWS]
    part1_ref[...] = parts[ROWS : 2 * ROWS]
    low = parts.astype(bf16)
    part2_ref[...] = low[2 * ROWS :]
    g_ref[ROWS:] = low
    theirs_ref[...] = (
        mm(held_ref[:HALF], g_ref[: 2 * ROWS])
        + mm(held1_ref[:HALF], g_ref[2 * ROWS : 3 * ROWS])
        + mm(held2_ref[:HALF], g_ref[3 * ROWS :])
    ).astype(bf16)


def own_kernel(held_ref, held1_ref, held2_ref, g_ref, w_ref, mine_ref, gq_ref):
    mine_ref[...] = (
        mm(held_ref[HALF:], g_ref[: 2 * ROWS])
        + mm(held1_ref[HALF:], g_ref[2 * ROWS : 3 * ROWS])
        + mm(held2_ref[HALF:], g_ref[3 * ROWS :])
    )
    gq_ref[...] = nt(g_ref[:ROWS], w_ref[...]).astype(bf16)


def plane_kernel(pieces_ref, out_ref):
    total = pieces_ref[0].astype(f32)
    for i in range(1, 16):
        total = total + pieces_ref[i].astype(f32)
    for k in range(8):
        out_ref[:, k, :] = total[:, k * 128 : (k + 1) * 128]


def passage_kernel(part_ref, back_ref, far_ref, w_ref, out_ref):
    gep = part_ref[...] + back_ref[...].astype(f32) + far_ref[...].astype(f32)
    out_ref[...] = nt(gep.astype(bf16), w_ref[...]).astype(bf16)


def shape(rows, columns, dtype):
    return jax.ShapeDtypeStruct((rows, columns), dtype)


def call(kernel, outs, *args, scratch=(), smem=0):
    flops = 2 * ROWS * WIDTH * WIDTH
    return pl.pallas_call(
        kernel,
        out_shape=outs,
        in_specs=[pl.BlockSpec(memory_space=pltpu.SMEM)] * smem
        + [pl.BlockSpec(memory_space=pltpu.VMEM)] * (len(args) - smem),
        out_specs=jax.tree.map(lambda _: pl.BlockSpec(memory_space=pltpu.VMEM), outs),
        scratch_shapes=list(scratch),
        compiler_params=pltpu.CompilerParams(vmem_limit_bytes=16 * 2**20),
        cost_estimate=pl.CostEstimate(flops=flops, bytes_accessed=2**20, transcendentals=0),
    )(*args)


def body(query_states, passage_states, loss_weights, positives, head_weight):
    hq = query_states[0]
    hp = passage_states[0]
    weight = loss_weights[0][:, None]
    local = (positives[0] % ROWS)[:, None]
    square = shape(ROWS, WIDTH, bf16)

    hp1 = shifted(hp, 1)
    hp2 = shifted(hp, 2)

    core = lax.axis_index("c").astype(jnp.int32).reshape(1)
    eq, ep0, pick, held = call(
        project_kernel,
        (square, square, shape(WIDTH, WIDTH, bf16), shape(WIDTH, 2 * ROWS, bf16)),
        core, hq, hp, head_weight,
        smem=1,
    )
    ep1, held1 = call(first_kernel, (square, shape(WIDTH, ROWS, bf16)), hp1, head_weight, pick)
    part0, part1, part2, grads, held2, theirs = call(
        grads_kernel,
        (
            shape(ROWS, WIDTH, f32), shape(ROWS, WIDTH, f32), square,
            shape(4 * ROWS, WIDTH, bf16), shape(WIDTH, ROWS, bf16), shape(HALF, WIDTH, bf16),
        ),
        hp2, head_weight, pick, eq, ep0, ep1, held, held1, weight, local,
        scratch=[pltpu.VMEM((3 * ROWS, WIDTH), bf16)],
    )
    swapped = lax.ppermute(theirs, "c", [(0, 1), (1, 0)])
    back2 = lax.ppermute(part2, CHIPS, chip_route(step_back))
    mine, grad_q = call(
        own_kernel, (shape(HALF, WIDTH, f32), square), held, held1, held2, grads, head_weight
    )
    chip = (mine + swapped).astype(bf16)

    pieces = lax.all_to_all(chip, PLANE, 0, 0, tiled=True)
    plane = call(
        plane_kernel, jax.ShapeDtypeStruct((32, 8, 128), f32), pieces.reshape(16, 32, WIDTH)
    )

    part1 = after(part1, plane)
    back2 = after(back2, plane)
    kept = jnp.where(lax.axis_index("y") == 3, 0.0, back2.astype(f32))
    carried = (kept + part1).astype(bf16)
    plane = after(plane, carried)
    back1 = shifted(carried, -1)
    far = lax.ppermute(back2, CHIPS, chip_route(relay_back))
    pieces = lax.all_to_all(plane.reshape(16, 16, 128), "z", 0, 0, tiled=True)
    grad_p = call(passage_kernel, square, part0, back1, far, head_weight)
    head_grad = jnp.sum(pieces.reshape(16, 16, 128), axis=0).reshape(2, 1024)
    return (grad_q[None], grad_p[None], head_grad)


def solution(mesh):
    fine = Mesh(mesh.devices.reshape(SIZES), AXES)
    in_specs = (P(DP, BATCH, None), P(DP, BATCH, None), P(DP, BATCH), P(DP, BATCH), P())
    out_specs = (P(DP, BATCH, None), P(DP, BATCH, None), P((*BATCH, *DP), None))
    return jax.shard_map(body, mesh=fine, in_specs=in_specs, out_specs=out_specs, check_vma=False)
```

```python
import jax
import jax.numpy as jnp
from jax import lax
from jax.experimental import pallas as pl
from jax.experimental.pallas import tpu as pltpu
from jax.sharding import Mesh, PartitionSpec as P

ROWS = 128
AXES = ("z", "xh", "y", "xl", "c")
SIZES = (16, 2, 4, 2, 2)
BATCH = ("z", "xh", "y")
CHIPS = ("z", "xh", "y", "xl")
PLANE = ("xh", "y", "xl")
DP = ("xl", "c")
WIDTH = 1024
HALF = WIDTH // 2

score_scale = 0.1
bf16 = jnp.bfloat16
f32 = jnp.float32


def shifted(block, distance):
    n = lax.axis_size(BATCH)
    return lax.ppermute(block, BATCH, [(i, (i + distance) % n) for i in range(n)])


def chip_index(x, y, z):
    x, y, z = x % 4, y % 4, z % 16
    return ((z * 2 + x // 2) * 4 + y) * 2 + x % 2


def chip_route(target):
    pairs = []
    for z in range(16):
        for y in range(4):
            for x in range(4):
                to = target(x, y, z)
                if to is not None:
                    pairs.append((chip_index(x, y, z), chip_index(*to)))
    return pairs


def step_back(x, y, z):
    return (x, y - 1, z) if y else (x - 1, 3, z)


def relay_back(x, y, z):
    return (x - 1, 2, z - (1 if (x + 1) % 4 < 2 else 0)) if y == 3 else None


def mm(a, b):
    return jnp.dot(a, b, preferred_element_type=f32)


def nt(a, b):
    return lax.dot_general(a, b, (((1,), (1,)), ((), ())), preferred_element_type=f32)


def make_pick(core, pick_ref):
    pos = lax.broadcasted_iota(jnp.int32, (WIDTH, 128), 0)
    lane = lax.broadcasted_iota(jnp.int32, (WIDTH, 128), 1)
    plane, z, t = (pos >> 5) & 15, (pos >> 1) & 15, pos & 1
    c = jnp.where(pos < HALF, 1 - core, core)
    row = z * 64 + (plane >> 3) * 32 + ((plane >> 1) & 3) * 8 + (plane & 1) * 4 + c * 2 + t
    for j in range(WIDTH // 128):
        pick_ref[:, j * 128 : (j + 1) * 128] = jnp.where(row == lane + j * 128, 1.0, 0.0).astype(bf16)


def project_kernel(core_ref, hq_ref, hp_ref, w_ref, eq_ref, ep_ref, held_ref, pick_ref):
    eq_ref[...] = mm(hq_ref[...], w_ref[...]).astype(bf16)
    ep_ref[...] = mm(hp_ref[...], w_ref[...]).astype(bf16)
    make_pick(core_ref[0], pick_ref)
    held_ref[:, :ROWS] = nt(pick_ref[...], hq_ref[...]).astype(bf16)
    held_ref[:, ROWS:] = nt(pick_ref[...], hp_ref[...]).astype(bf16)


def grads_kernel(
    core_ref, hp1_ref, hp2_ref, w_ref, eq_ref, ep0_ref, held_ref, weight_ref, local_ref,
    part2_ref, g_ref, far_ref, theirs_ref, near_ref, ep_ref, pick_ref,
):
    near_ref[:ROWS] = hp1_ref[...]
    near_ref[ROWS:] = hp2_ref[...]
    ep_ref[:ROWS] = ep0_ref[...]
    ep_ref[ROWS:] = mm(near_ref[...], w_ref[...]).astype(bf16)
    make_pick(core_ref[0], pick_ref)
    far_ref[...] = nt(pick_ref[...], near_ref[...]).astype(bf16)
    scores = nt(eq_ref[...], ep_ref[...]) * score_scale
    top = jnp.max(scores, axis=1, keepdims=True)
    lse = top + jnp.log(jnp.sum(jnp.exp(scores - top), axis=1, keepdims=True))
    column = lax.broadcasted_iota(jnp.int32, (ROWS, 3 * ROWS), 1)
    onehot = jnp.where(column == local_ref[...], 1.0, 0.0)
    ds = (weight_ref[...] * score_scale * (jnp.exp(scores - lse) - onehot)).astype(bf16)
    g_ref[:ROWS] = mm(ds, ep_ref[...]).astype(bf16)
    parts = mm(ds.astype(f32).T.astype(bf16), eq_ref[...]).astype(bf16)
    part2_ref[...] = parts[2 * ROWS :]
    g_ref[ROWS:] = parts
    theirs_ref[...] = (
        mm(held_ref[:HALF], g_ref[: 2 * ROWS]) + mm(far_ref[:HALF], g_ref[2 * ROWS :])
    ).astype(bf16)


def own_kernel(held_ref, far_ref, g_ref, w_ref, mine_ref, gq_ref, part0_ref, part1_ref):
    part0_ref[...] = g_ref[ROWS : 2 * ROWS]
    part1_ref[...] = g_ref[2 * ROWS : 3 * ROWS]
    mine_ref[...] = mm(held_ref[HALF:], g_ref[: 2 * ROWS]) + mm(far_ref[HALF:], g_ref[2 * ROWS :])
    gq_ref[...] = nt(g_ref[:ROWS], w_ref[...]).astype(bf16)


def join_kernel(mine_ref, swapped_ref, out_ref):
    out_ref[...] = (mine_ref[...] + swapped_ref[...].astype(f32)).astype(bf16)


def plane_kernel(pieces_ref, out_ref):
    total = pieces_ref[0].astype(f32)
    for i in range(1, 16):
        total = total + pieces_ref[i].astype(f32)
    for k in range(8):
        out_ref[:, k, :] = total[:, k * 128 : (k + 1) * 128]


def passage_kernel(part_ref, back_ref, far_ref, w_ref, out_ref):
    gep = part_ref[...].astype(f32) + back_ref[...].astype(f32) + far_ref[...].astype(f32)
    out_ref[...] = nt(gep.astype(bf16), w_ref[...]).astype(bf16)


def shape(rows, columns, dtype):
    return jax.ShapeDtypeStruct((rows, columns), dtype)


def call(kernel, outs, *args, scratch=(), smem=0, weighs=1):
    flops = weighs * 2 * ROWS * WIDTH * WIDTH
    return pl.pallas_call(
        kernel,
        out_shape=outs,
        in_specs=[pl.BlockSpec(memory_space=pltpu.SMEM)] * smem
        + [pl.BlockSpec(memory_space=pltpu.VMEM)] * (len(args) - smem),
        out_specs=jax.tree.map(lambda _: pl.BlockSpec(memory_space=pltpu.VMEM), outs),
        scratch_shapes=list(scratch),
        compiler_params=pltpu.CompilerParams(vmem_limit_bytes=16 * 2**20),
        cost_estimate=pl.CostEstimate(flops=flops, bytes_accessed=2**20, transcendentals=0),
    )(*args)


def body(query_states, passage_states, loss_weights, positives, head_weight):
    hq = query_states[0]
    hp = passage_states[0]
    weight = loss_weights[0][:, None]
    local = (positives[0] % ROWS)[:, None]
    square = shape(ROWS, WIDTH, bf16)

    hp1 = shifted(hp, 1)
    hp2 = shifted(hp, 2)

    core = lax.axis_index("c").astype(jnp.int32).reshape(1)
    eq, ep0, held = call(
        project_kernel,
        (square, square, shape(WIDTH, 2 * ROWS, bf16)),
        core, hq, hp, head_weight,
        smem=1, scratch=[pltpu.VMEM((WIDTH, WIDTH), bf16)],
    )
    part2, grads, far, theirs = call(
        grads_kernel,
        (square, shape(4 * ROWS, WIDTH, bf16), shape(WIDTH, 2 * ROWS, bf16), shape(HALF, WIDTH, bf16)),
        core, hp1, hp2, head_weight, eq, ep0, held, weight, local,
        smem=1,
        scratch=[
            pltpu.VMEM((2 * ROWS, WIDTH), bf16),
            pltpu.VMEM((3 * ROWS, WIDTH), bf16),
            pltpu.VMEM((WIDTH, WIDTH), bf16),
        ],
    )
    swapped = lax.ppermute(theirs, "c", [(0, 1), (1, 0)])
    back2 = lax.ppermute(part2, CHIPS, chip_route(step_back))
    mine, grad_q, part0, part1 = call(
        own_kernel, (shape(HALF, WIDTH, f32), square, square, square), held, far, grads, head_weight
    )
    chip = call(join_kernel, shape(HALF, WIDTH, bf16), mine, swapped)
    kept = jnp.where(lax.axis_index("y") == 3, 0.0, back2.astype(f32))
    carried = (kept + part1.astype(f32)).astype(bf16)
    chip, carried, back2 = lax.optimization_barrier((chip, carried, back2))

    pieces = lax.all_to_all(chip, PLANE, 0, 0, tiled=True)
    pieces, carried, back2 = lax.optimization_barrier((pieces, carried, back2))
    back1 = shifted(carried, -1)
    across = lax.ppermute(back2, CHIPS, chip_route(relay_back))
    plane = call(
        plane_kernel, jax.ShapeDtypeStruct((32, 8, 128), f32), pieces.reshape(16, 32, WIDTH)
    )
    pieces = lax.all_to_all(plane.reshape(16, 16, 128), "z", 0, 0, tiled=True)
    grad_p = call(passage_kernel, square, part0, back1, across, head_weight, weighs=20)
    head_grad = jnp.sum(pieces.reshape(16, 16, 128), axis=0).reshape(2, 1024)
    return (grad_q[None], grad_p[None], head_grad)


def solution(mesh):
    fine = Mesh(mesh.devices.reshape(SIZES), AXES)
    in_specs = (P(DP, BATCH, None), P(DP, BATCH, None), P(DP, BATCH), P(DP, BATCH), P())
    out_specs = (P(DP, BATCH, None), P(DP, BATCH, None), P((*BATCH, *DP), None))
    return jax.shard_map(body, mesh=fine, in_specs=in_specs, out_specs=out_specs, check_vma=False)
```

```python
import jax
import jax.numpy as jnp
from jax import lax
from jax.experimental import pallas as pl
from jax.experimental.pallas import tpu as pltpu
from jax.sharding import Mesh, PartitionSpec as P

ROWS = 128
AXES = ("z", "xh", "y", "xl", "c")
SIZES = (16, 2, 4, 2, 2)
BATCH = ("z", "xh", "y")
CHIPS = ("z", "xh", "y", "xl")
PLANE = ("xh", "xl", "y")
DP = ("xl", "c")
WIDTH = 1024
HALF = WIDTH // 2

score_scale = 0.1
bf16 = jnp.bfloat16
f32 = jnp.float32


def shifted(block, distance):
    n = lax.axis_size(BATCH)
    return lax.ppermute(block, BATCH, [(i, (i + distance) % n) for i in range(n)])


def chip_index(x, y, z):
    x, y, z = x % 4, y % 4, z % 16
    return ((z * 2 + x // 2) * 4 + y) * 2 + x % 2


def chip_route(target):
    pairs = []
    for z in range(16):
        for y in range(4):
            for x in range(4):
                to = target(x, y, z)
                if to is not None:
                    pairs.append((chip_index(x, y, z), chip_index(*to)))
    return pairs


def step_back(x, y, z):
    return (x, y - 1, z) if y else (x - 1, 3, z)


def relay_back(x, y, z):
    return (x - 1, 2, z - (1 if (x + 1) % 4 < 2 else 0)) if y == 3 else None


def mm(a, b):
    return jnp.dot(a, b, preferred_element_type=f32)


def nt(a, b):
    return lax.dot_general(a, b, (((1,), (1,)), ((), ())), preferred_element_type=f32)


def make_pick(core, pick_ref):
    pos = lax.broadcasted_iota(jnp.int32, (WIDTH, 128), 0)
    lane = lax.broadcasted_iota(jnp.int32, (WIDTH, 128), 1)
    plane, z, t = (pos >> 5) & 15, (pos >> 1) & 15, pos & 1
    c = jnp.where(pos < HALF, 1 - core, core)
    row = z * 64 + (plane >> 3) * 32 + (plane & 3) * 8 + ((plane >> 2) & 1) * 4 + c * 2 + t
    for j in range(WIDTH // 128):
        pick_ref[:, j * 128 : (j + 1) * 128] = jnp.where(row == lane + j * 128, 1.0, 0.0).astype(bf16)


def project_kernel(core_ref, hq_ref, hp_ref, w_ref, eq_ref, ep_ref, held_ref, pick_ref):
    eq_ref[...] = mm(hq_ref[...], w_ref[...]).astype(bf16)
    ep_ref[...] = mm(hp_ref[...], w_ref[...]).astype(bf16)
    make_pick(core_ref[0], pick_ref)
    held_ref[:, :ROWS] = nt(pick_ref[...], hq_ref[...]).astype(bf16)
    held_ref[:, ROWS:] = nt(pick_ref[...], hp_ref[...]).astype(bf16)


def grads_kernel(
    core_ref, w_ref, eq_ref, ep0_ref, held_ref, weight_ref, local_ref, hp1_ref, hp2_ref,
    gq_ref, part0_ref, part1_ref, part2_ref, theirs_ref, mine_ref,
    near_ref, ep_ref, pick_ref, far_ref, g_ref, sems,
):
    first = pltpu.make_async_copy(hp1_ref, near_ref.at[:ROWS], sems.at[0])
    second = pltpu.make_async_copy(hp2_ref, near_ref.at[ROWS:], sems.at[1])
    first.start()
    second.start()
    ep_ref[:ROWS] = ep0_ref[...]
    make_pick(core_ref[0], pick_ref)
    first.wait()
    second.wait()
    ep_ref[ROWS:] = mm(near_ref[...], w_ref[...]).astype(bf16)
    scores = nt(eq_ref[...], ep_ref[...]) * score_scale
    far_ref[...] = nt(pick_ref[...], near_ref[...]).astype(bf16)
    top = jnp.max(scores, axis=1, keepdims=True)
    lse = top + jnp.log(jnp.sum(jnp.exp(scores - top), axis=1, keepdims=True))
    column = lax.broadcasted_iota(jnp.int32, (ROWS, 3 * ROWS), 1)
    onehot = jnp.where(column == local_ref[...], 1.0, 0.0)
    ds = (weight_ref[...] * score_scale * (jnp.exp(scores - lse) - onehot)).astype(bf16)
    gq = mm(ds, ep_ref[...]).astype(bf16)
    gq_ref[...] = gq
    g_ref[:ROWS] = gq
    parts = mm(ds.astype(f32).T.astype(bf16), eq_ref[...]).astype(bf16)
    g_ref[ROWS:] = parts
    part0_ref[...] = parts[:ROWS]
    part1_ref[...] = parts[ROWS : 2 * ROWS]
    part2_ref[...] = parts[2 * ROWS :]
    theirs_ref[...] = (
        mm(held_ref[:HALF], g_ref[: 2 * ROWS]) + mm(far_ref[:HALF], g_ref[2 * ROWS :])
    ).astype(bf16)
    mine_ref[...] = mm(held_ref[HALF:], g_ref[: 2 * ROWS]) + mm(far_ref[HALF:], g_ref[2 * ROWS :])


def query_kernel(gq_ref, w_ref, out_ref):
    out_ref[...] = nt(gq_ref[...], w_ref[...]).astype(bf16)


def join_kernel(mine_ref, swapped_ref, out_ref):
    out_ref[...] = (mine_ref[...] + swapped_ref[...].astype(f32)).astype(bf16)


def plane_kernel(pieces_ref, out_ref):
    total = pieces_ref[0].astype(f32)
    for i in range(1, 16):
        total = total + pieces_ref[i].astype(f32)
    for k in range(8):
        out_ref[:, k, :] = total[:, k * 128 : (k + 1) * 128]


def passage_kernel(part_ref, back_ref, far_ref, w_ref, out_ref):
    gep = part_ref[...].astype(f32) + back_ref[...].astype(f32) + far_ref[...].astype(f32)
    out_ref[...] = nt(gep.astype(bf16), w_ref[...]).astype(bf16)


def shape(rows, columns, dtype):
    return jax.ShapeDtypeStruct((rows, columns), dtype)


def call(kernel, outs, *args, scratch=(), smem=0, anywhere=0, weighs=1):
    vmem = len(args) - smem - anywhere
    return pl.pallas_call(
        kernel,
        out_shape=outs,
        in_specs=[pl.BlockSpec(memory_space=pltpu.SMEM)] * smem
        + [pl.BlockSpec(memory_space=pltpu.VMEM)] * vmem
        + [pl.BlockSpec(memory_space=pl.ANY)] * anywhere,
        out_specs=jax.tree.map(lambda _: pl.BlockSpec(memory_space=pltpu.VMEM), outs),
        scratch_shapes=list(scratch),
        compiler_params=pltpu.CompilerParams(vmem_limit_bytes=16 * 2**20),
        cost_estimate=pl.CostEstimate(
            flops=weighs * 2 * ROWS * WIDTH * WIDTH, bytes_accessed=2**20, transcendentals=0
        ),
    )(*args)


def body(query_states, passage_states, loss_weights, positives, head_weight):
    hq = query_states[0]
    hp = passage_states[0]
    weight = loss_weights[0][:, None]
    local = (positives[0] % ROWS)[:, None]
    square = shape(ROWS, WIDTH, bf16)

    hp1 = shifted(hp, 1)
    hp2 = shifted(hp, 2)

    core = lax.axis_index("c").astype(jnp.int32).reshape(1)
    eq, ep0, held = call(
        project_kernel,
        (square, square, shape(WIDTH, 2 * ROWS, bf16)),
        core, hq, hp, head_weight,
        smem=1, scratch=[pltpu.VMEM((WIDTH, WIDTH), bf16)],
    )
    gq, part0, part1, part2, theirs, mine = call(
        grads_kernel,
        (square, square, square, square, shape(HALF, WIDTH, bf16), shape(HALF, WIDTH, f32)),
        core, head_weight, eq, ep0, held, weight, local, hp1, hp2,
        smem=1, anywhere=2,
        scratch=[
            pltpu.VMEM((2 * ROWS, WIDTH), bf16),
            pltpu.VMEM((3 * ROWS, WIDTH), bf16),
            pltpu.VMEM((WIDTH, WIDTH), bf16),
            pltpu.VMEM((WIDTH, 2 * ROWS), bf16),
            pltpu.VMEM((4 * ROWS, WIDTH), bf16),
            pltpu.SemaphoreType.DMA((2,)),
        ],
    )
    swapped = lax.ppermute(theirs, "c", [(0, 1), (1, 0)])
    chip = call(join_kernel, shape(HALF, WIDTH, bf16), mine, swapped)
    pieces = lax.all_to_all(chip, PLANE, 0, 0, tiled=True)
    part2, gq, chip = lax.optimization_barrier((part2, gq, chip))
    back2 = lax.ppermute(part2, CHIPS, chip_route(step_back))
    grad_q = call(query_kernel, square, gq, head_weight)
    kept = jnp.where(lax.axis_index("y") == 3, 0.0, back2.astype(f32))
    carried = (kept + part1.astype(f32)).astype(bf16)
    back1 = shifted(carried, -1)
    across = lax.ppermute(back2, CHIPS, chip_route(relay_back))
    pieces, carried, back2 = lax.optimization_barrier((pieces, carried, back2))
    plane = call(
        plane_kernel, jax.ShapeDtypeStruct((32, 8, 128), f32), pieces.reshape(16, 32, WIDTH)
    )
    pieces = lax.all_to_all(plane.reshape(16, 16, 128), "z", 0, 0, tiled=True)
    grad_p = call(passage_kernel, square, part0, back1, across, head_weight, weighs=20)
    head_grad = jnp.sum(pieces.reshape(16, 16, 128), axis=0).reshape(2, 1024)
    return (grad_q[None], grad_p[None], head_grad)


def solution(mesh):
    fine = Mesh(mesh.devices.reshape(SIZES), AXES)
    in_specs = (P(DP, BATCH, None), P(DP, BATCH, None), P(DP, BATCH), P(DP, BATCH), P())
    out_specs = (P(DP, BATCH, None), P(DP, BATCH, None), P((*BATCH, *DP), None))
    return jax.shard_map(body, mesh=fine, in_specs=in_specs, out_specs=out_specs, check_vma=False)
```

```python
import jax
import jax.numpy as jnp
from jax import lax
from jax.experimental import pallas as pl
from jax.experimental.pallas import tpu as pltpu
from jax.sharding import Mesh, PartitionSpec as P

ROWS = 128
AXES = ("z", "xh", "y", "xl", "c")
SIZES = (16, 2, 4, 2, 2)
BATCH = ("z", "xh", "y")
PLANE = ("xh", "xl", "y")
DP = ("xl", "c")
WIDTH = 1024
HALF = WIDTH // 2

VMEM = pl.BlockSpec(memory_space=pltpu.VMEM)
ANY = pl.BlockSpec(memory_space=pl.ANY)
HBM = pl.BlockSpec(memory_space=pltpu.HBM)

score_scale = 0.1
bf16 = jnp.bfloat16
f32 = jnp.float32


def shifted(block, distance):
    n = lax.axis_size(BATCH)
    return lax.ppermute(block, BATCH, [(i, (i + distance) % n) for i in range(n)])


def mm(a, b):
    return jnp.dot(a, b, preferred_element_type=f32)


def nt(a, b):
    return lax.dot_general(a, b, (((1,), (1,)), ((), ())), preferred_element_type=f32)


def make_pick(core, pick_ref):
    pos = lax.broadcasted_iota(jnp.int32, (WIDTH, 128), 0)
    lane = lax.broadcasted_iota(jnp.int32, (WIDTH, 128), 1)
    plane, z, t = (pos >> 5) & 15, (pos >> 1) & 15, pos & 1
    c = jnp.where(pos < HALF, 1 - core, core)
    row = z * 64 + (plane >> 3) * 32 + (plane & 3) * 8 + ((plane >> 2) & 1) * 4 + c * 2 + t
    for j in range(WIDTH // 128):
        pick_ref[:, j * 128 : (j + 1) * 128] = jnp.where(row == lane + j * 128, 1.0, 0.0).astype(bf16)


def project_kernel(core_ref, hq_ref, hp_ref, w_ref, eq_ref, ep_ref, held_ref, pick_ref):
    eq_ref[...] = mm(hq_ref[...], w_ref[...]).astype(bf16)
    ep_ref[...] = mm(hp_ref[...], w_ref[...]).astype(bf16)
    make_pick(core_ref[0], pick_ref)
    held_ref[:, :ROWS] = nt(pick_ref[...], hq_ref[...]).astype(bf16)
    held_ref[:, ROWS:] = nt(pick_ref[...], hp_ref[...]).astype(bf16)


def grads_kernel(
    core_ref, w_ref, eq_ref, ep0_ref, held_ref, weight_ref, local_ref, hp1_ref, hp2_ref,
    note_ref, gq_ref, part_ref, theirs_ref, mine_ref,
    near_ref, ep_ref, pick_ref, far_ref, g_ref, part_keep, note_keep, sems,
):
    first = pltpu.make_async_copy(hp1_ref, near_ref.at[:ROWS], sems.at[0])
    second = pltpu.make_async_copy(hp2_ref, near_ref.at[ROWS:], sems.at[1])
    first.start()
    second.start()
    ep_ref[:ROWS] = ep0_ref[...]
    make_pick(core_ref[0], pick_ref)
    first.wait()
    second.wait()
    ep_ref[ROWS:] = mm(near_ref[...], w_ref[...]).astype(bf16)
    scores = nt(eq_ref[...], ep_ref[...]) * score_scale
    far_ref[...] = nt(pick_ref[...], near_ref[...]).astype(bf16)
    top = jnp.max(scores, axis=1, keepdims=True)
    lse = top + jnp.log(jnp.sum(jnp.exp(scores - top), axis=1, keepdims=True))
    column = lax.broadcasted_iota(jnp.int32, (ROWS, 3 * ROWS), 1)
    onehot = jnp.where(column == local_ref[...], 1.0, 0.0)
    ds = (weight_ref[...] * score_scale * (jnp.exp(scores - lse) - onehot)).astype(bf16)
    which = lax.broadcasted_iota(jnp.int32, (ROWS, ROWS), 1)
    note = jnp.where(which == 0, lse, jnp.where(which == 1, weight_ref[...] * score_scale, 0.0))
    note_keep[...] = note.T[:8]
    g_ref[:ROWS] = mm(ds, ep_ref[...]).astype(bf16)
    parts = mm(ds.astype(f32).T.astype(bf16), eq_ref[...])
    part_keep[...] = parts[:ROWS]
    out = [
        pltpu.make_async_copy(note_keep, note_ref, sems.at[2]),
        pltpu.make_async_copy(g_ref.at[:ROWS], gq_ref, sems.at[3]),
        pltpu.make_async_copy(part_keep, part_ref, sems.at[4]),
    ]
    for copy in out:
        copy.start()
    g_ref[ROWS:] = parts.astype(bf16)
    theirs_ref[...] = (
        mm(held_ref[:HALF], g_ref[: 2 * ROWS]) + mm(far_ref[:HALF], g_ref[2 * ROWS :])
    ).astype(bf16)
    mine_ref[...] = mm(held_ref[HALF:], g_ref[: 2 * ROWS]) + mm(far_ref[HALF:], g_ref[2 * ROWS :])
    for copy in out:
        copy.wait()


def query_kernel(gq_ref, w_ref, out_ref):
    out_ref[...] = nt(gq_ref[...], w_ref[...]).astype(bf16)


def later_kernel(hq1_ref, hq2_ref, w_ref, hp_ref, eq_ref, scores_ref, both_ref):
    both_ref[:ROWS] = hq1_ref[...]
    both_ref[ROWS:] = hq2_ref[...]
    eq_ref[...] = mm(both_ref[...], w_ref[...]).astype(bf16)
    ep = mm(hp_ref[...], w_ref[...]).astype(bf16)
    scores_ref[...] = nt(ep, eq_ref[...]) * score_scale


def passage_kernel(part_ref, eq_ref, scores_ref, note1_ref, note2_ref, w_ref, out_ref):
    gep = part_ref[...]
    for k, note_ref in enumerate((note1_ref, note2_ref)):
        own = slice(k * ROWS, (k + 1) * ROWS)
        ds = note_ref[1:2, :] * jnp.exp(scores_ref[:, own] - note_ref[0:1, :])
        gep = gep + mm(ds.astype(bf16), eq_ref[own])
    out_ref[...] = nt(gep.astype(bf16), w_ref[...]).astype(bf16)


def join_kernel(mine_ref, swapped_ref, out_ref, sum_ref, sems):
    copies = []
    for i in range(4):
        rows = slice(i * ROWS, (i + 1) * ROWS)
        sum_ref[rows] = (mine_ref[rows] + swapped_ref[rows].astype(f32)).astype(bf16)
        copies.append(pltpu.make_async_copy(sum_ref.at[rows], out_ref.at[rows], sems.at[i]))
        copies[i].start()
    for copy in copies:
        copy.wait()


def plane_kernel(pieces_ref, out_ref):
    total = pieces_ref[0].astype(f32)
    for i in range(1, 16):
        total = total + pieces_ref[i].astype(f32)
    for k in range(8):
        out_ref[:, k, :] = total[:, k * 128 : (k + 1) * 128]


def shape(rows, columns, dtype):
    return jax.ShapeDtypeStruct((rows, columns), dtype)


def call(kernel, outs, *args, scratch=(), smem=0, anywhere=0, weighs=1, out_specs=None):
    if out_specs is None:
        out_specs = jax.tree.map(lambda _: VMEM, outs)
    vmem = len(args) - smem - anywhere
    return pl.pallas_call(
        kernel,
        out_shape=outs,
        in_specs=[pl.BlockSpec(memory_space=pltpu.SMEM)] * smem
        + [VMEM] * vmem
        + [ANY] * anywhere,
        out_specs=out_specs,
        scratch_shapes=list(scratch),
        compiler_params=pltpu.CompilerParams(vmem_limit_bytes=16 * 2**20),
        cost_estimate=pl.CostEstimate(
            flops=weighs * 2 * ROWS * WIDTH * WIDTH, bytes_accessed=2**20, transcendentals=0
        ),
    )(*args)


def body(query_states, passage_states, loss_weights, positives, head_weight):
    hq = query_states[0]
    hp = passage_states[0]
    weight = loss_weights[0][:, None]
    local = (positives[0] % ROWS)[:, None]
    square = shape(ROWS, WIDTH, bf16)

    hp1 = shifted(hp, 1)
    hp2 = shifted(hp, 2)

    core = lax.axis_index("c").astype(jnp.int32).reshape(1)
    eq, ep0, held = call(
        project_kernel,
        (square, square, shape(WIDTH, 2 * ROWS, bf16)),
        core, hq, hp, head_weight,
        smem=1, scratch=[pltpu.VMEM((WIDTH, WIDTH), bf16)],
    )
    late, eq = lax.optimization_barrier((hq, eq))
    hq1 = shifted(late, -1)
    hq2 = shifted(late, -2)
    note, gq, part, theirs, mine = call(
        grads_kernel,
        (shape(8, ROWS, f32), square, shape(ROWS, WIDTH, f32), shape(HALF, WIDTH, bf16), shape(HALF, WIDTH, f32)),
        core, head_weight, eq, ep0, held, weight, local, hp1, hp2,
        smem=1, anywhere=2, out_specs=(HBM, HBM, HBM, VMEM, VMEM),
        scratch=[
            pltpu.VMEM((2 * ROWS, WIDTH), bf16),
            pltpu.VMEM((3 * ROWS, WIDTH), bf16),
            pltpu.VMEM((WIDTH, WIDTH), bf16),
            pltpu.VMEM((WIDTH, 2 * ROWS), bf16),
            pltpu.VMEM((4 * ROWS, WIDTH), bf16),
            pltpu.VMEM((ROWS, WIDTH), f32),
            pltpu.VMEM((8, ROWS), f32),
            pltpu.SemaphoreType.DMA((5,)),
        ],
    )
    theirs, hq1, hq2 = lax.optimization_barrier((theirs, hq1, hq2))
    swapped = lax.ppermute(theirs, "c", [(0, 1), (1, 0)])
    chip = call(
        join_kernel, shape(HALF, WIDTH, bf16), mine, swapped, out_specs=HBM,
        scratch=[pltpu.VMEM((HALF, WIDTH), bf16), pltpu.SemaphoreType.DMA((4,))],
    )
    chip, note, gq = lax.optimization_barrier((chip, note, gq))
    pieces = lax.all_to_all(chip, PLANE, 0, 0, tiled=True)
    note1 = shifted(note, -1)
    note2 = shifted(note, -2)
    grad_q = call(query_kernel, square, gq, head_weight)
    eq12, scores = call(
        later_kernel, (shape(2 * ROWS, WIDTH, bf16), shape(ROWS, 2 * ROWS, f32)), hq1, hq2, head_weight, hp,
        scratch=[pltpu.VMEM((2 * ROWS, WIDTH), bf16)],
    )
    plane = call(
        plane_kernel, jax.ShapeDtypeStruct((32, 8, 128), f32), pieces.reshape(16, 32, WIDTH)
    )
    pieces = lax.all_to_all(plane.reshape(16, 16, 128), "z", 0, 0, tiled=True)
    grad_p = call(passage_kernel, square, part, eq12, scores, note1, note2, head_weight, weighs=20)
    head_grad = jnp.sum(pieces.reshape(16, 16, 128), axis=0).reshape(2, 1024)
    return (grad_q[None], grad_p[None], head_grad)


def solution(mesh):
    fine = Mesh(mesh.devices.reshape(SIZES), AXES)
    in_specs = (P(DP, BATCH, None), P(DP, BATCH, None), P(DP, BATCH), P(DP, BATCH), P())
    out_specs = (P(DP, BATCH, None), P(DP, BATCH, None), P((*BATCH, *DP), None))
    return jax.shard_map(body, mesh=fine, in_specs=in_specs, out_specs=out_specs, check_vma=False)
```

```python
import jax
import jax.numpy as jnp
from jax import lax
from jax.experimental import pallas as pl
from jax.experimental.pallas import tpu as pltpu
from jax.sharding import Mesh, PartitionSpec as P

ROWS = 128
AXES = ("z", "xh", "y", "xl", "c")
SIZES = (16, 2, 4, 2, 2)
BATCH = ("z", "xh", "y")
PLANE = ("xh", "xl", "y")
DP = ("xl", "c")
WIDTH = 1024
HALF = WIDTH // 2

VMEM = pl.BlockSpec(memory_space=pltpu.VMEM)
HBM = pl.BlockSpec(memory_space=pltpu.HBM)

score_scale = 0.1
bf16 = jnp.bfloat16
f32 = jnp.float32


def shifted(block, distance):
    n = lax.axis_size(BATCH)
    return lax.ppermute(block, BATCH, [(i, (i + distance) % n) for i in range(n)])


def mm(a, b):
    return jnp.dot(a, b, preferred_element_type=f32)


def nt(a, b):
    return lax.dot_general(a, b, (((1,), (1,)), ((), ())), preferred_element_type=f32)


def make_pick(core, pick_ref):
    pos = lax.broadcasted_iota(jnp.int32, (WIDTH, 128), 0)
    lane = lax.broadcasted_iota(jnp.int32, (WIDTH, 128), 1)
    plane, z, t = (pos >> 5) & 15, (pos >> 1) & 15, pos & 1
    c = jnp.where(pos < HALF, 1 - core, core)
    row = z * 64 + (plane >> 3) * 32 + (plane & 3) * 8 + ((plane >> 2) & 1) * 4 + c * 2 + t
    for j in range(WIDTH // 128):
        pick_ref[:, j * 128 : (j + 1) * 128] = jnp.where(row == lane + j * 128, 1.0, 0.0).astype(bf16)


def grads_kernel(
    core_ref, weight_ref, local_ref, hq_any, hp_any, hp1_any, hp2_any, w_any,
    note_ref, gq_ref, theirs_any, mine_any,
    states_ref, e_ref, pick_ref, held_ref, g_ref, note_keep, w_ref, theirs_ref, mine_ref, sems,
):
    into = [
        pltpu.make_async_copy(block, states_ref.at[i * ROWS : (i + 1) * ROWS], sems.at[i])
        for i, block in enumerate((hq_any, hp_any, hp1_any, hp2_any))
    ]
    into.append(pltpu.make_async_copy(w_any, w_ref, sems.at[6]))
    for copy in into:
        copy.start()
    make_pick(core_ref[0], pick_ref)
    for copy in into:
        copy.wait()
    e_ref[...] = mm(states_ref[...], w_ref[...]).astype(bf16)
    scores = nt(e_ref[:ROWS], e_ref[ROWS:]) * score_scale
    held_ref[...] = nt(pick_ref[...], states_ref[...]).astype(bf16)
    top = jnp.max(scores, axis=1, keepdims=True)
    lse = top + jnp.log(jnp.sum(jnp.exp(scores - top), axis=1, keepdims=True))
    column = lax.broadcasted_iota(jnp.int32, (ROWS, 3 * ROWS), 1)
    onehot = jnp.where(column == local_ref[...], 1.0, 0.0)
    ds = (weight_ref[...] * score_scale * (jnp.exp(scores - lse) - onehot)).astype(bf16)
    which = lax.broadcasted_iota(jnp.int32, (ROWS, ROWS), 1)
    note = jnp.where(which == 0, lse, jnp.where(which == 1, weight_ref[...] * score_scale, 0.0))
    note_keep[...] = note.T[:8]
    g_ref[:ROWS] = mm(ds, e_ref[ROWS:]).astype(bf16)
    out = [
        pltpu.make_async_copy(note_keep, note_ref, sems.at[4]),
        pltpu.make_async_copy(g_ref.at[:ROWS], gq_ref, sems.at[5]),
    ]
    for copy in out:
        copy.start()
    g_ref[ROWS:] = mm(ds.astype(f32).T.astype(bf16), e_ref[:ROWS]).astype(bf16)
    for i in range(4):
        rows = slice(i * ROWS, (i + 1) * ROWS)
        theirs_ref[rows] = mm(held_ref[rows], g_ref[...]).astype(bf16)
        out.append(pltpu.make_async_copy(theirs_ref.at[rows], theirs_any.at[rows], sems.at[7 + i]))
        out[-1].start()
    for i in range(4):
        rows = slice(i * ROWS, (i + 1) * ROWS)
        mine_ref[rows] = mm(held_ref[HALF + i * ROWS : HALF + (i + 1) * ROWS], g_ref[...])
        out.append(pltpu.make_async_copy(mine_ref.at[rows], mine_any.at[rows], sems.at[11 + i]))
        out[-1].start()
    for copy in out:
        copy.wait()


def query_kernel(gq_ref, w_ref, out_ref):
    out_ref[...] = nt(gq_ref[...], w_ref[...]).astype(bf16)


def later_kernel(hq_ref, hq1_ref, hq2_ref, w_ref, hp_ref, eq_ref, scores_ref, all_ref):
    all_ref[:ROWS] = hq_ref[...]
    all_ref[ROWS : 2 * ROWS] = hq1_ref[...]
    all_ref[2 * ROWS :] = hq2_ref[...]
    eq_ref[...] = mm(all_ref[...], w_ref[...]).astype(bf16)
    ep = mm(hp_ref[...], w_ref[...]).astype(bf16)
    scores_ref[...] = nt(ep, eq_ref[...]) * score_scale


def passage_kernel(local_ref, eq_ref, scores_ref, note0_ref, note1_ref, note2_ref, w_ref, out_ref):
    passage = lax.broadcasted_iota(jnp.int32, (ROWS, ROWS), 0)
    onehot = jnp.where(passage == local_ref[...], 1.0, 0.0)
    gep = jnp.zeros((ROWS, WIDTH), f32)
    for k, note_ref in enumerate((note0_ref, note1_ref, note2_ref)):
        own = slice(k * ROWS, (k + 1) * ROWS)
        p = jnp.exp(scores_ref[:, own] - note_ref[0:1, :])
        ds = note_ref[1:2, :] * (p - onehot if k == 0 else p)
        gep = gep + mm(ds.astype(bf16), eq_ref[own])
    out_ref[...] = nt(gep.astype(bf16), w_ref[...]).astype(bf16)


def join_kernel(mine_ref, swapped_ref, out_ref, sum_ref, sems):
    copies = []
    for i in range(4):
        rows = slice(i * ROWS, (i + 1) * ROWS)
        sum_ref[rows] = (mine_ref[rows] + swapped_ref[rows].astype(f32)).astype(bf16)
        copies.append(pltpu.make_async_copy(sum_ref.at[rows], out_ref.at[rows], sems.at[i]))
        copies[i].start()
    for copy in copies:
        copy.wait()


def plane_kernel(pieces_ref, out_ref):
    total = pieces_ref[0].astype(f32)
    for i in range(1, 16):
        total = total + pieces_ref[i].astype(f32)
    for k in range(8):
        out_ref[:, k, :] = total[:, k * 128 : (k + 1) * 128]


def shape(rows, columns, dtype):
    return jax.ShapeDtypeStruct((rows, columns), dtype)


def call(kernel, outs, *args, scratch=(), smem=0, anywhere=0, weighs=1, out_specs=None, limit=16):
    if out_specs is None:
        out_specs = jax.tree.map(lambda _: VMEM, outs)
    vmem = len(args) - smem - anywhere
    return pl.pallas_call(
        kernel,
        out_shape=outs,
        in_specs=[pl.BlockSpec(memory_space=pltpu.SMEM)] * smem
        + [VMEM] * vmem
        + [HBM] * anywhere,
        out_specs=out_specs,
        scratch_shapes=list(scratch),
        compiler_params=pltpu.CompilerParams(vmem_limit_bytes=limit * 2**20),
        cost_estimate=pl.CostEstimate(
            flops=weighs * 2 * ROWS * WIDTH * WIDTH, bytes_accessed=2**20, transcendentals=0
        ),
    )(*args)


def body(query_states, passage_states, loss_weights, positives, head_weight):
    hq = query_states[0]
    hp = passage_states[0]
    weight = loss_weights[0][:, None]
    local = (positives[0] % ROWS)[:, None]
    square = shape(ROWS, WIDTH, bf16)

    hp1 = shifted(hp, 1)
    hp2 = shifted(hp, 2)
    hq2 = shifted(hq, -2)
    hq1 = shifted(hq, -1)

    core = lax.axis_index("c").astype(jnp.int32).reshape(1)
    note, gq, theirs, mine = call(
        grads_kernel,
        (shape(8, ROWS, f32), square, shape(HALF, WIDTH, bf16), shape(HALF, WIDTH, f32)),
        core, weight, local, hq, hp, hp1, hp2, head_weight,
        smem=1, anywhere=5, out_specs=(HBM, HBM, HBM, HBM), limit=56,
        scratch=[
            pltpu.VMEM((4 * ROWS, WIDTH), bf16),
            pltpu.VMEM((4 * ROWS, WIDTH), bf16),
            pltpu.VMEM((WIDTH, WIDTH), bf16),
            pltpu.VMEM((WIDTH, 4 * ROWS), bf16),
            pltpu.VMEM((4 * ROWS, WIDTH), bf16),
            pltpu.VMEM((8, ROWS), f32),
            pltpu.VMEM((WIDTH, WIDTH), bf16),
            pltpu.VMEM((HALF, WIDTH), bf16),
            pltpu.VMEM((HALF, WIDTH), f32),
            pltpu.SemaphoreType.DMA((15,)),
        ],
    )
    theirs, hq1, hq2 = lax.optimization_barrier((theirs, hq1, hq2))
    swapped = lax.ppermute(theirs, "c", [(0, 1), (1, 0)])
    chip = call(
        join_kernel, shape(HALF, WIDTH, bf16), mine, swapped, out_specs=HBM,
        scratch=[pltpu.VMEM((HALF, WIDTH), bf16), pltpu.SemaphoreType.DMA((4,))],
    )
    pieces = lax.all_to_all(chip, PLANE, 0, 0, tiled=True)
    plane = call(
        plane_kernel, jax.ShapeDtypeStruct((32, 8, 128), f32), pieces.reshape(16, 32, WIDTH)
    )
    plane, note, gq, hq, hq1, hq2, hp = lax.optimization_barrier((plane, note, gq, hq, hq1, hq2, hp))
    pieces = lax.all_to_all(plane.reshape(16, 16, 128), "z", 0, 0, tiled=True)
    note1 = shifted(note, -1)
    note2 = shifted(note, -2)
    eq3, scores = call(
        later_kernel,
        (shape(3 * ROWS, WIDTH, bf16), shape(ROWS, 3 * ROWS, f32)),
        hq, hq1, hq2, head_weight, hp,
        scratch=[pltpu.VMEM((3 * ROWS, WIDTH), bf16)],
    )
    grad_q = call(query_kernel, square, gq, head_weight)
    row = positives % ROWS
    grad_p = call(passage_kernel, square, row, eq3, scores, note, note1, note2, head_weight)
    head_grad = jnp.sum(pieces.reshape(16, 16, 128), axis=0).reshape(2, 1024)
    return (grad_q[None], grad_p[None], head_grad)


def solution(mesh):
    fine = Mesh(mesh.devices.reshape(SIZES), AXES)
    in_specs = (P(DP, BATCH, None), P(DP, BATCH, None), P(DP, BATCH), P(DP, BATCH), P())
    out_specs = (P(DP, BATCH, None), P(DP, BATCH, None), P((*BATCH, *DP), None))
    return jax.shard_map(body, mesh=fine, in_specs=in_specs, out_specs=out_specs, check_vma=False)
```

```python
import jax
import jax.numpy as jnp
from jax import lax
from jax.experimental import pallas as pl
from jax.experimental.pallas import tpu as pltpu
from jax.sharding import Mesh, PartitionSpec as P

ROWS = 128
AXES = ("z", "xh", "y", "xl", "c")
SIZES = (16, 2, 4, 2, 2)
BATCH = ("z", "xh", "y")
PLANE = ("xh", "xl", "y")
DP = ("xl", "c")
WIDTH = 1024
HALF = WIDTH // 2

VMEM = pl.BlockSpec(memory_space=pltpu.VMEM)
HBM = pl.BlockSpec(memory_space=pltpu.HBM)

score_scale = 0.1
bf16 = jnp.bfloat16
f32 = jnp.float32


def shifted(block, distance):
    n = lax.axis_size(BATCH)
    return lax.ppermute(block, BATCH, [(i, (i + distance) % n) for i in range(n)])


def mm(a, b):
    return jnp.dot(a, b, preferred_element_type=f32)


def nt(a, b):
    return lax.dot_general(a, b, (((1,), (1,)), ((), ())), preferred_element_type=f32)


def make_pick(core, pick_ref):
    pos = lax.broadcasted_iota(jnp.int32, (WIDTH, 128), 0)
    lane = lax.broadcasted_iota(jnp.int32, (WIDTH, 128), 1)
    plane, z, t = (pos >> 5) & 15, (pos >> 1) & 15, pos & 1
    c = jnp.where(pos < HALF, 1 - core, core)
    row = z * 64 + (plane >> 3) * 32 + (plane & 3) * 8 + ((plane >> 2) & 1) * 4 + c * 2 + t
    for j in range(WIDTH // 128):
        pick_ref[:, j * 128 : (j + 1) * 128] = jnp.where(row == lane + j * 128, 1.0, 0.0).astype(bf16)


def grads_kernel(
    core_ref, weight_ref, local_ref, hq_any, hp_any, hp1_any, hp2_any, w_any,
    note_any, gq_any, theirs_any, own_any, g_any,
    states_ref, e_ref, pick_ref, held_ref, g_ref, note_keep, w_ref, theirs_ref, sems,
):
    into = [
        pltpu.make_async_copy(block, states_ref.at[i * ROWS : (i + 1) * ROWS], sems.at[i])
        for i, block in enumerate((hq_any, hp_any, hp1_any, hp2_any))
    ]
    into.append(pltpu.make_async_copy(w_any, w_ref, sems.at[6]))
    for copy in into:
        copy.start()
    make_pick(core_ref[0], pick_ref)
    for copy in into:
        copy.wait()
    e_ref[...] = mm(states_ref[...], w_ref[...]).astype(bf16)
    scores = nt(e_ref[:ROWS], e_ref[ROWS:]) * score_scale
    held_ref[...] = nt(pick_ref[...], states_ref[...]).astype(bf16)
    top = jnp.max(scores, axis=1, keepdims=True)
    lse = top + jnp.log(jnp.sum(jnp.exp(scores - top), axis=1, keepdims=True))
    column = lax.broadcasted_iota(jnp.int32, (ROWS, 3 * ROWS), 1)
    onehot = jnp.where(column == local_ref[...], 1.0, 0.0)
    ds = (weight_ref[...] * score_scale * (jnp.exp(scores - lse) - onehot)).astype(bf16)
    which = lax.broadcasted_iota(jnp.int32, (ROWS, ROWS), 1)
    note = jnp.where(which == 0, lse, jnp.where(which == 1, weight_ref[...] * score_scale, 0.0))
    note_keep[...] = note.T[:8]
    g_ref[:ROWS] = mm(ds, e_ref[ROWS:]).astype(bf16)
    g_ref[ROWS:] = mm(ds.astype(f32).T.astype(bf16), e_ref[:ROWS]).astype(bf16)
    out = [
        pltpu.make_async_copy(note_keep, note_any, sems.at[4]),
        pltpu.make_async_copy(g_ref.at[:ROWS], gq_any, sems.at[5]),
        pltpu.make_async_copy(held_ref.at[HALF:], own_any, sems.at[7]),
        pltpu.make_async_copy(g_ref, g_any, sems.at[8]),
    ]
    for copy in out:
        copy.start()
    for i in range(2):
        rows = slice(i * HALF // 2, (i + 1) * HALF // 2)
        theirs_ref[rows] = mm(held_ref[rows], g_ref[...]).astype(bf16)
        out.append(pltpu.make_async_copy(theirs_ref.at[rows], theirs_any.at[rows], sems.at[9 + i]))
        out[-1].start()
    for copy in out:
        copy.wait()


def own_kernel(held_ref, g_ref, mine_ref):
    mine_ref[...] = mm(held_ref[...], g_ref[...])


def query_kernel(gq_ref, w_ref, out_ref):
    out_ref[...] = nt(gq_ref[...], w_ref[...]).astype(bf16)


def later_kernel(hq_ref, hq1_ref, hq2_ref, w_ref, hp_ref, eq_ref, scores_ref, all_ref):
    all_ref[:ROWS] = hq_ref[...]
    all_ref[ROWS : 2 * ROWS] = hq1_ref[...]
    all_ref[2 * ROWS :] = hq2_ref[...]
    eq_ref[...] = mm(all_ref[...], w_ref[...]).astype(bf16)
    ep = mm(hp_ref[...], w_ref[...]).astype(bf16)
    scores_ref[...] = nt(ep, eq_ref[...]) * score_scale


def passage_kernel(local_ref, eq_ref, scores_ref, note0_ref, note1_ref, note2_ref, w_ref, out_ref):
    passage = lax.broadcasted_iota(jnp.int32, (ROWS, ROWS), 0)
    onehot = jnp.where(passage == local_ref[...], 1.0, 0.0)
    gep = jnp.zeros((ROWS, WIDTH), f32)
    for k, note_ref in enumerate((note0_ref, note1_ref, note2_ref)):
        own = slice(k * ROWS, (k + 1) * ROWS)
        p = jnp.exp(scores_ref[:, own] - note_ref[0:1, :])
        ds = note_ref[1:2, :] * (p - onehot if k == 0 else p)
        gep = gep + mm(ds.astype(bf16), eq_ref[own])
    out_ref[...] = nt(gep.astype(bf16), w_ref[...]).astype(bf16)


def join_kernel(mine_ref, swapped_ref, out_ref, sum_ref, sems):
    copies = []
    for i in range(4):
        rows = slice(i * ROWS, (i + 1) * ROWS)
        sum_ref[rows] = (mine_ref[rows] + swapped_ref[rows].astype(f32)).astype(bf16)
        copies.append(pltpu.make_async_copy(sum_ref.at[rows], out_ref.at[rows], sems.at[i]))
        copies[i].start()
    for copy in copies:
        copy.wait()


def plane_kernel(pieces_ref, out_ref):
    total = pieces_ref[0].astype(f32)
    for i in range(1, 16):
        total = total + pieces_ref[i].astype(f32)
    for k in range(8):
        out_ref[:, k, :] = total[:, k * 128 : (k + 1) * 128]


def shape(rows, columns, dtype):
    return jax.ShapeDtypeStruct((rows, columns), dtype)


def call(kernel, outs, *args, scratch=(), smem=0, anywhere=0, weighs=1, out_specs=None, limit=16):
    if out_specs is None:
        out_specs = jax.tree.map(lambda _: VMEM, outs)
    vmem = len(args) - smem - anywhere
    return pl.pallas_call(
        kernel,
        out_shape=outs,
        in_specs=[pl.BlockSpec(memory_space=pltpu.SMEM)] * smem
        + [VMEM] * vmem
        + [HBM] * anywhere,
        out_specs=out_specs,
        scratch_shapes=list(scratch),
        compiler_params=pltpu.CompilerParams(vmem_limit_bytes=limit * 2**20),
        cost_estimate=pl.CostEstimate(
            flops=weighs * 2 * ROWS * WIDTH * WIDTH, bytes_accessed=2**20, transcendentals=0
        ),
    )(*args)


def body(query_states, passage_states, loss_weights, positives, head_weight):
    hq = query_states[0]
    hp = passage_states[0]
    weight = loss_weights[0][:, None]
    local = (positives[0] % ROWS)[:, None]
    square = shape(ROWS, WIDTH, bf16)

    hp1 = shifted(hp, 1)
    hp2 = shifted(hp, 2)
    hq2 = shifted(hq, -2)
    hq1 = shifted(hq, -1)

    core = lax.axis_index("c").astype(jnp.int32).reshape(1)
    half = shape(HALF, WIDTH, bf16)
    note, gq, theirs, own, grads = call(
        grads_kernel,
        (shape(8, ROWS, f32), square, half, shape(HALF, 4 * ROWS, bf16), shape(4 * ROWS, WIDTH, bf16)),
        core, weight, local, hq, hp, hp1, hp2, head_weight,
        smem=1, anywhere=5, out_specs=(HBM,) * 5, limit=56,
        scratch=[
            pltpu.VMEM((4 * ROWS, WIDTH), bf16),
            pltpu.VMEM((4 * ROWS, WIDTH), bf16),
            pltpu.VMEM((WIDTH, WIDTH), bf16),
            pltpu.VMEM((WIDTH, 4 * ROWS), bf16),
            pltpu.VMEM((4 * ROWS, WIDTH), bf16),
            pltpu.VMEM((8, ROWS), f32),
            pltpu.VMEM((WIDTH, WIDTH), bf16),
            pltpu.VMEM((HALF, WIDTH), bf16),
            pltpu.SemaphoreType.DMA((11,)),
        ],
    )
    theirs, hq1, hq2 = lax.optimization_barrier((theirs, hq1, hq2))
    swapped = lax.ppermute(theirs, "c", [(0, 1), (1, 0)])
    mine = call(own_kernel, shape(HALF, WIDTH, f32), own, grads)
    chip = call(
        join_kernel, shape(HALF, WIDTH, bf16), mine, swapped, out_specs=HBM,
        scratch=[pltpu.VMEM((HALF, WIDTH), bf16), pltpu.SemaphoreType.DMA((4,))],
    )
    pieces = lax.all_to_all(chip, PLANE, 0, 0, tiled=True)
    plane = call(
        plane_kernel, jax.ShapeDtypeStruct((32, 8, 128), f32), pieces.reshape(16, 32, WIDTH)
    )
    plane, note, gq, hq, hq1, hq2, hp = lax.optimization_barrier((plane, note, gq, hq, hq1, hq2, hp))
    pieces = lax.all_to_all(plane.reshape(16, 16, 128), "z", 0, 0, tiled=True)
    note1 = shifted(note, -1)
    note2 = shifted(note, -2)
    eq3, scores = call(
        later_kernel,
        (shape(3 * ROWS, WIDTH, bf16), shape(ROWS, 3 * ROWS, f32)),
        hq, hq1, hq2, head_weight, hp,
        scratch=[pltpu.VMEM((3 * ROWS, WIDTH), bf16)],
    )
    grad_q = call(query_kernel, square, gq, head_weight)
    row = positives % ROWS
    grad_p = call(passage_kernel, square, row, eq3, scores, note, note1, note2, head_weight)
    head_grad = jnp.sum(pieces.reshape(16, 16, 128), axis=0).reshape(2, 1024)
    return (grad_q[None], grad_p[None], head_grad)


def solution(mesh):
    fine = Mesh(mesh.devices.reshape(SIZES), AXES)
    in_specs = (P(DP, BATCH, None), P(DP, BATCH, None), P(DP, BATCH), P(DP, BATCH), P())
    out_specs = (P(DP, BATCH, None), P(DP, BATCH, None), P((*BATCH, *DP), None))
    return jax.shard_map(body, mesh=fine, in_specs=in_specs, out_specs=out_specs, check_vma=False)
```

```python
import jax
import jax.numpy as jnp
from jax import lax
from jax.experimental import pallas as pl
from jax.experimental.pallas import tpu as pltpu
from jax.sharding import Mesh, PartitionSpec as P

ROWS = 128
AXES = ("z", "xh", "y", "xl", "c")
SIZES = (16, 2, 4, 2, 2)
BATCH = ("z", "xh", "y")
PLANE = ("xh", "xl", "y")
DP = ("xl", "c")
WIDTH = 1024
HALF = WIDTH // 2

VMEM = pl.BlockSpec(memory_space=pltpu.VMEM)
HBM = pl.BlockSpec(memory_space=pltpu.HBM)

score_scale = 0.1
bf16 = jnp.bfloat16
f32 = jnp.float32


def shifted(block, distance):
    n = lax.axis_size(BATCH)
    return lax.ppermute(block, BATCH, [(i, (i + distance) % n) for i in range(n)])


def mm(a, b):
    return jnp.dot(a, b, preferred_element_type=f32)


def nt(a, b):
    return lax.dot_general(a, b, (((1,), (1,)), ((), ())), preferred_element_type=f32)


def make_pick(core, pick_ref):
    pos = lax.broadcasted_iota(jnp.int32, (WIDTH, 128), 0)
    lane = lax.broadcasted_iota(jnp.int32, (WIDTH, 128), 1)
    plane, z, t = (pos >> 5) & 15, (pos >> 1) & 15, pos & 1
    c = jnp.where(pos < HALF, 1 - core, core)
    row = z * 64 + (plane >> 3) * 32 + (plane & 3) * 8 + ((plane >> 2) & 1) * 4 + c * 2 + t
    for j in range(WIDTH // 128):
        pick_ref[:, j * 128 : (j + 1) * 128] = jnp.where(row == lane + j * 128, 1.0, 0.0).astype(bf16)


def grads_kernel(
    core_ref, weight_ref, local_ref, hq_any, hp_any, hp1_any, hp2_any, w_any,
    note_any, gq_any, theirs_any, own_any, g_any,
    states_ref, e_ref, pick_ref, held_ref, g_ref, note_keep, w_ref, theirs_ref, sems,
):
    into = [
        pltpu.make_async_copy(block, states_ref.at[i * ROWS : (i + 1) * ROWS], sems.at[i])
        for i, block in enumerate((hq_any, hp_any, hp1_any, hp2_any))
    ]
    into.append(pltpu.make_async_copy(w_any, w_ref, sems.at[6]))
    for copy in into:
        copy.start()
    make_pick(core_ref[0], pick_ref)
    for copy in into:
        copy.wait()
    e_ref[...] = mm(states_ref[...], w_ref[...]).astype(bf16)
    scores = nt(e_ref[:ROWS], e_ref[ROWS:]) * score_scale
    held_ref[...] = nt(pick_ref[...], states_ref[...]).astype(bf16)
    top = jnp.max(scores, axis=1, keepdims=True)
    lse = top + jnp.log(jnp.sum(jnp.exp(scores - top), axis=1, keepdims=True))
    column = lax.broadcasted_iota(jnp.int32, (ROWS, 3 * ROWS), 1)
    onehot = jnp.where(column == local_ref[...], 1.0, 0.0)
    ds = (weight_ref[...] * score_scale * (jnp.exp(scores - lse) - onehot)).astype(bf16)
    which = lax.broadcasted_iota(jnp.int32, (ROWS, ROWS), 1)
    note = jnp.where(which == 0, lse, jnp.where(which == 1, weight_ref[...] * score_scale, 0.0))
    note_keep[...] = note.T[:8]
    g_ref[:ROWS] = mm(ds, e_ref[ROWS:]).astype(bf16)
    g_ref[ROWS:] = mm(ds.astype(f32).T.astype(bf16), e_ref[:ROWS]).astype(bf16)
    out = [
        pltpu.make_async_copy(note_keep, note_any, sems.at[4]),
        pltpu.make_async_copy(g_ref.at[:ROWS], gq_any, sems.at[5]),
        pltpu.make_async_copy(held_ref.at[HALF:], own_any, sems.at[7]),
        pltpu.make_async_copy(g_ref, g_any, sems.at[8]),
    ]
    for copy in out:
        copy.start()
    for i in range(2):
        rows = slice(i * HALF // 2, (i + 1) * HALF // 2)
        theirs_ref[rows] = mm(held_ref[rows], g_ref[...]).astype(bf16)
        out.append(pltpu.make_async_copy(theirs_ref.at[rows], theirs_any.at[rows], sems.at[9 + i]))
        out[-1].start()
    for copy in out:
        copy.wait()


def own_kernel(held_ref, g_ref, mine_ref):
    mine_ref[...] = mm(held_ref[...], g_ref[...])


def query_kernel(gq_ref, w_ref, out_ref):
    out_ref[...] = nt(gq_ref[...], w_ref[...]).astype(bf16)


def later_kernel(hq_ref, hq1_ref, hq2_ref, w_ref, hp_ref, eq_ref, scores_ref, all_ref):
    all_ref[:ROWS] = hq_ref[...]
    all_ref[ROWS : 2 * ROWS] = hq1_ref[...]
    all_ref[2 * ROWS :] = hq2_ref[...]
    eq_ref[...] = mm(all_ref[...], w_ref[...]).astype(bf16)
    ep = mm(hp_ref[...], w_ref[...]).astype(bf16)
    scores_ref[...] = nt(ep, eq_ref[...]) * score_scale


def passage_kernel(local_ref, eq_ref, scores_ref, note0_ref, note1_ref, note2_ref, w_ref, out_ref):
    passage = lax.broadcasted_iota(jnp.int32, (ROWS, ROWS), 0)
    onehot = jnp.where(passage == local_ref[...], 1.0, 0.0)
    gep = jnp.zeros((ROWS, WIDTH), f32)
    for k, note_ref in enumerate((note0_ref, note1_ref, note2_ref)):
        own = slice(k * ROWS, (k + 1) * ROWS)
        p = jnp.exp(scores_ref[:, own] - note_ref[0:1, :])
        ds = note_ref[1:2, :] * (p - onehot if k == 0 else p)
        gep = gep + mm(ds.astype(bf16), eq_ref[own])
    out_ref[...] = nt(gep.astype(bf16), w_ref[...]).astype(bf16)


def join_kernel(mine_ref, swapped_ref, out_ref, sum_ref, sems):
    copies = []
    for i in range(4):
        rows = slice(i * ROWS, (i + 1) * ROWS)
        sum_ref[rows] = (mine_ref[rows] + swapped_ref[rows].astype(f32)).astype(bf16)
        copies.append(pltpu.make_async_copy(sum_ref.at[rows], out_ref.at[rows], sems.at[i]))
        copies[i].start()
    for copy in copies:
        copy.wait()


def plane_kernel(pieces_ref, out_ref):
    total = pieces_ref[0].astype(f32)
    for i in range(1, 16):
        total = total + pieces_ref[i].astype(f32)
    for k in range(8):
        out_ref[:, k, :] = total[:, k * 128 : (k + 1) * 128]


def shape(rows, columns, dtype):
    return jax.ShapeDtypeStruct((rows, columns), dtype)


def call(kernel, outs, *args, scratch=(), smem=0, anywhere=0, weighs=1, out_specs=None, limit=16):
    if out_specs is None:
        out_specs = jax.tree.map(lambda _: VMEM, outs)
    vmem = len(args) - smem - anywhere
    return pl.pallas_call(
        kernel,
        out_shape=outs,
        in_specs=[pl.BlockSpec(memory_space=pltpu.SMEM)] * smem
        + [VMEM] * vmem
        + [HBM] * anywhere,
        out_specs=out_specs,
        scratch_shapes=list(scratch),
        compiler_params=pltpu.CompilerParams(vmem_limit_bytes=limit * 2**20),
        cost_estimate=pl.CostEstimate(
            flops=weighs * 2 * ROWS * WIDTH * WIDTH, bytes_accessed=2**20, transcendentals=0
        ),
    )(*args)


def body(query_states, passage_states, loss_weights, positives, head_weight):
    hq = query_states[0]
    hp = passage_states[0]
    weight = loss_weights[0][:, None]
    local = (positives[0] % ROWS)[:, None]
    square = shape(ROWS, WIDTH, bf16)

    hp1 = shifted(hp, 1)
    hp2 = shifted(hp, 2)
    hq2 = shifted(hq, -2)
    hq1 = shifted(hq, -1)

    core = lax.axis_index("c").astype(jnp.int32).reshape(1)
    half = shape(HALF, WIDTH, bf16)
    note, gq, theirs, own, grads = call(
        grads_kernel,
        (shape(8, ROWS, f32), square, half, shape(HALF, 4 * ROWS, bf16), shape(4 * ROWS, WIDTH, bf16)),
        core, weight, local, hq, hp, hp1, hp2, head_weight,
        smem=1, anywhere=5, out_specs=(HBM,) * 5, limit=56,
        scratch=[
            pltpu.VMEM((4 * ROWS, WIDTH), bf16),
            pltpu.VMEM((4 * ROWS, WIDTH), bf16),
            pltpu.VMEM((WIDTH, WIDTH), bf16),
            pltpu.VMEM((WIDTH, 4 * ROWS), bf16),
            pltpu.VMEM((4 * ROWS, WIDTH), bf16),
            pltpu.VMEM((8, ROWS), f32),
            pltpu.VMEM((WIDTH, WIDTH), bf16),
            pltpu.VMEM((HALF, WIDTH), bf16),
            pltpu.SemaphoreType.DMA((11,)),
        ],
    )
    theirs, hq1, hq2 = lax.optimization_barrier((theirs, hq1, hq2))
    swapped = lax.ppermute(theirs, "c", [(0, 1), (1, 0)])
    mine = call(own_kernel, shape(HALF, WIDTH, f32), own, grads)
    chip = call(
        join_kernel, shape(HALF, WIDTH, bf16), mine, swapped, out_specs=HBM,
        scratch=[pltpu.VMEM((HALF, WIDTH), bf16), pltpu.SemaphoreType.DMA((4,))],
    )
    chip, note, gq = lax.optimization_barrier((chip, note, gq))
    pieces = lax.all_to_all(chip, PLANE, 0, 0, tiled=True)
    note1 = shifted(note, -1)
    note2 = shifted(note, -2)
    eq3, scores = call(
        later_kernel,
        (shape(3 * ROWS, WIDTH, bf16), shape(ROWS, 3 * ROWS, f32)),
        hq, hq1, hq2, head_weight, hp,
        scratch=[pltpu.VMEM((3 * ROWS, WIDTH), bf16)],
    )
    grad_q = call(query_kernel, square, gq, head_weight)
    row = positives % ROWS
    grad_p = call(
        passage_kernel, square, row, eq3, scores, note, note1, note2, head_weight
    )
    pieces, grad_p, grad_q = lax.optimization_barrier((pieces, grad_p, grad_q))
    plane = call(
        plane_kernel, jax.ShapeDtypeStruct((32, 8, 128), f32), pieces.reshape(16, 32, WIDTH)
    )
    pieces = lax.all_to_all(plane.reshape(16, 16, 128), "z", 0, 0, tiled=True)
    head_grad = jnp.sum(pieces.reshape(16, 16, 128), axis=0).reshape(2, 1024)
    return (grad_q[None], grad_p[None], head_grad)


def solution(mesh):
    fine = Mesh(mesh.devices.reshape(SIZES), AXES)
    in_specs = (P(DP, BATCH, None), P(DP, BATCH, None), P(DP, BATCH), P(DP, BATCH), P())
    out_specs = (P(DP, BATCH, None), P(DP, BATCH, None), P((*BATCH, *DP), None))
    return jax.shard_map(body, mesh=fine, in_specs=in_specs, out_specs=out_specs, check_vma=False)
```

```python
import jax
import jax.numpy as jnp
from jax import lax
from jax.experimental import pallas as pl
from jax.experimental.pallas import tpu as pltpu
from jax.sharding import Mesh, PartitionSpec as P

ROWS = 128
AXES = ("z", "xh", "y", "xl", "c")
SIZES = (16, 2, 4, 2, 2)
BATCH = ("z", "xh", "y")
PLANE = ("xh", "xl", "y")
DP = ("xl", "c")
WIDTH = 1024
HALF = WIDTH // 2

VMEM = pl.BlockSpec(memory_space=pltpu.VMEM)
HBM = pl.BlockSpec(memory_space=pltpu.HBM)

score_scale = 0.1
bf16 = jnp.bfloat16
f32 = jnp.float32


def shifted(block, distance):
    n = lax.axis_size(BATCH)
    return lax.ppermute(block, BATCH, [(i, (i + distance) % n) for i in range(n)])


def mm(a, b):
    return jnp.dot(a, b, preferred_element_type=f32)


def nt(a, b):
    return lax.dot_general(a, b, (((1,), (1,)), ((), ())), preferred_element_type=f32)


def make_pick(core, pick_ref):
    pos = lax.broadcasted_iota(jnp.int32, (WIDTH, 128), 0)
    lane = lax.broadcasted_iota(jnp.int32, (WIDTH, 128), 1)
    plane, z, t = (pos >> 5) & 15, (pos >> 1) & 15, pos & 1
    c = jnp.where(pos < HALF, 1 - core, core)
    row = z * 64 + (plane >> 3) * 32 + (plane & 3) * 8 + ((plane >> 2) & 1) * 4 + c * 2 + t
    for j in range(WIDTH // 128):
        pick_ref[:, j * 128 : (j + 1) * 128] = jnp.where(row == lane + j * 128, 1.0, 0.0).astype(bf16)


def upright(row):
    return jnp.broadcast_to(row, (ROWS, ROWS)).T[:, :1]


def grads_kernel(
    core_ref, weight_ref, positive_ref, hq_any, hp_any, hp1_any, hp2_any, w_any,
    note_any, gq_any, theirs_any, own_any, g_any,
    states_ref, e_ref, pick_ref, held_ref, g_ref, note_keep, w_ref, theirs_ref, sems,
):
    into = [
        pltpu.make_async_copy(block, states_ref.at[i * ROWS : (i + 1) * ROWS], sems.at[i])
        for i, block in enumerate((hq_any, hp_any, hp1_any, hp2_any))
    ]
    into.append(pltpu.make_async_copy(w_any, w_ref, sems.at[6]))
    for copy in into:
        copy.start()
    weight = upright(weight_ref[...])
    local = upright((positive_ref[...] & (ROWS - 1)).astype(f32)).astype(jnp.int32)
    make_pick(core_ref[0], pick_ref)
    for copy in into:
        copy.wait()
    e_ref[...] = mm(states_ref[...], w_ref[...]).astype(bf16)
    scores = nt(e_ref[:ROWS], e_ref[ROWS:]) * score_scale
    held_ref[...] = nt(pick_ref[...], states_ref[...]).astype(bf16)
    top = jnp.max(scores, axis=1, keepdims=True)
    lse = top + jnp.log(jnp.sum(jnp.exp(scores - top), axis=1, keepdims=True))
    column = lax.broadcasted_iota(jnp.int32, (ROWS, 3 * ROWS), 1)
    onehot = jnp.where(column == local, 1.0, 0.0)
    ds = (weight * score_scale * (jnp.exp(scores - lse) - onehot)).astype(bf16)
    which = lax.broadcasted_iota(jnp.int32, (ROWS, ROWS), 1)
    note = jnp.where(which == 0, lse, jnp.where(which == 1, weight * score_scale, 0.0))
    note_keep[...] = note.T[:8]
    g_ref[:ROWS] = mm(ds, e_ref[ROWS:]).astype(bf16)
    g_ref[ROWS:] = mm(ds.astype(f32).T.astype(bf16), e_ref[:ROWS]).astype(bf16)
    out = [
        pltpu.make_async_copy(note_keep, note_any, sems.at[4]),
        pltpu.make_async_copy(g_ref.at[:ROWS], gq_any, sems.at[5]),
        pltpu.make_async_copy(held_ref.at[HALF:], own_any, sems.at[7]),
        pltpu.make_async_copy(g_ref, g_any, sems.at[8]),
    ]
    for copy in out:
        copy.start()
    for i in range(2):
        rows = slice(i * HALF // 2, (i + 1) * HALF // 2)
        theirs_ref[rows] = mm(held_ref[rows], g_ref[...]).astype(bf16)
        out.append(pltpu.make_async_copy(theirs_ref.at[rows], theirs_any.at[rows], sems.at[9 + i]))
        out[-1].start()
    for copy in out:
        copy.wait()


def own_kernel(held_ref, g_ref, mine_ref):
    mine_ref[...] = mm(held_ref[...], g_ref[...])


def query_kernel(gq_ref, w_ref, out_ref):
    out_ref[...] = nt(gq_ref[...], w_ref[...]).astype(bf16)


def later_kernel(hq_ref, hq1_ref, hq2_ref, w_ref, hp_ref, eq_ref, scores_ref, all_ref):
    all_ref[:ROWS] = hq_ref[...]
    all_ref[ROWS : 2 * ROWS] = hq1_ref[...]
    all_ref[2 * ROWS :] = hq2_ref[...]
    eq_ref[...] = mm(all_ref[...], w_ref[...]).astype(bf16)
    ep = mm(hp_ref[...], w_ref[...]).astype(bf16)
    scores_ref[...] = nt(ep, eq_ref[...]) * score_scale


def passage_kernel(positive_ref, eq_ref, scores_ref, note0_ref, note1_ref, note2_ref, w_ref, out_ref):
    passage = lax.broadcasted_iota(jnp.int32, (ROWS, ROWS), 0)
    onehot = jnp.where(passage == (positive_ref[...] & (ROWS - 1)), 1.0, 0.0)
    gep = jnp.zeros((ROWS, WIDTH), f32)
    for k, note_ref in enumerate((note0_ref, note1_ref, note2_ref)):
        own = slice(k * ROWS, (k + 1) * ROWS)
        p = jnp.exp(scores_ref[:, own] - note_ref[0:1, :])
        ds = note_ref[1:2, :] * (p - onehot if k == 0 else p)
        gep = gep + mm(ds.astype(bf16), eq_ref[own])
    out_ref[...] = nt(gep.astype(bf16), w_ref[...]).astype(bf16)


def join_kernel(mine_ref, swapped_ref, out_ref, sum_ref, sems):
    copies = []
    for i in range(4):
        rows = slice(i * ROWS, (i + 1) * ROWS)
        sum_ref[rows] = (mine_ref[rows] + swapped_ref[rows].astype(f32)).astype(bf16)
        copies.append(pltpu.make_async_copy(sum_ref.at[rows], out_ref.at[rows], sems.at[i]))
        copies[i].start()
    for copy in copies:
        copy.wait()


def plane_kernel(pieces_ref, out_ref):
    total = pieces_ref[0].astype(f32)
    for i in range(1, 16):
        total = total + pieces_ref[i].astype(f32)
    for k in range(8):
        out_ref[:, k, :] = total[:, k * 128 : (k + 1) * 128]


def shape(rows, columns, dtype):
    return jax.ShapeDtypeStruct((rows, columns), dtype)


def call(kernel, outs, *args, scratch=(), smem=0, anywhere=0, weighs=1, out_specs=None, limit=16):
    if out_specs is None:
        out_specs = jax.tree.map(lambda _: VMEM, outs)
    vmem = len(args) - smem - anywhere
    return pl.pallas_call(
        kernel,
        out_shape=outs,
        in_specs=[pl.BlockSpec(memory_space=pltpu.SMEM)] * smem
        + [VMEM] * vmem
        + [HBM] * anywhere,
        out_specs=out_specs,
        scratch_shapes=list(scratch),
        compiler_params=pltpu.CompilerParams(vmem_limit_bytes=limit * 2**20),
        cost_estimate=pl.CostEstimate(
            flops=weighs * 2 * ROWS * WIDTH * WIDTH, bytes_accessed=2**20, transcendentals=0
        ),
    )(*args)


def body(query_states, passage_states, loss_weights, positives, head_weight):
    hq = query_states[0]
    hp = passage_states[0]
    square = shape(ROWS, WIDTH, bf16)

    hp1 = shifted(hp, 1)
    hp2 = shifted(hp, 2)
    hq2 = shifted(hq, -2)
    hq1 = shifted(hq, -1)

    core = lax.axis_index("c").astype(jnp.int32).reshape(1)
    half = shape(HALF, WIDTH, bf16)
    note, gq, theirs, own, grads = call(
        grads_kernel,
        (shape(8, ROWS, f32), square, half, shape(HALF, 4 * ROWS, bf16), shape(4 * ROWS, WIDTH, bf16)),
        core, loss_weights, positives, hq, hp, hp1, hp2, head_weight,
        smem=1, anywhere=5, out_specs=(HBM,) * 5, limit=56,
        scratch=[
            pltpu.VMEM((4 * ROWS, WIDTH), bf16),
            pltpu.VMEM((4 * ROWS, WIDTH), bf16),
            pltpu.VMEM((WIDTH, WIDTH), bf16),
            pltpu.VMEM((WIDTH, 4 * ROWS), bf16),
            pltpu.VMEM((4 * ROWS, WIDTH), bf16),
            pltpu.VMEM((8, ROWS), f32),
            pltpu.VMEM((WIDTH, WIDTH), bf16),
            pltpu.VMEM((HALF, WIDTH), bf16),
            pltpu.SemaphoreType.DMA((11,)),
        ],
    )
    theirs, hq1, hq2 = lax.optimization_barrier((theirs, hq1, hq2))
    swapped = lax.ppermute(theirs, "c", [(0, 1), (1, 0)])
    mine = call(own_kernel, shape(HALF, WIDTH, f32), own, grads)
    chip = call(
        join_kernel, shape(HALF, WIDTH, bf16), mine, swapped, out_specs=HBM,
        scratch=[pltpu.VMEM((HALF, WIDTH), bf16), pltpu.SemaphoreType.DMA((4,))],
    )
    pieces = lax.all_to_all(chip, PLANE, 0, 0, tiled=True)
    plane = call(
        plane_kernel, jax.ShapeDtypeStruct((32, 8, 128), f32), pieces.reshape(16, 32, WIDTH)
    )
    plane, note, gq, hq, hq1, hq2, hp = lax.optimization_barrier((plane, note, gq, hq, hq1, hq2, hp))
    pieces = lax.all_to_all(plane.reshape(16, 16, 128), "z", 0, 0, tiled=True)
    note1 = shifted(note, -1)
    note2 = shifted(note, -2)
    eq3, scores = call(
        later_kernel,
        (shape(3 * ROWS, WIDTH, bf16), shape(ROWS, 3 * ROWS, f32)),
        hq, hq1, hq2, head_weight, hp,
        scratch=[pltpu.VMEM((3 * ROWS, WIDTH), bf16)],
    )
    grad_q = call(query_kernel, square, gq, head_weight)
    grad_p = call(passage_kernel, square, positives, eq3, scores, note, note1, note2, head_weight)
    head_grad = jnp.sum(pieces.reshape(16, 16, 128), axis=0).reshape(2, 1024)
    return (grad_q[None], grad_p[None], head_grad)


def solution(mesh):
    fine = Mesh(mesh.devices.reshape(SIZES), AXES)
    in_specs = (P(DP, BATCH, None), P(DP, BATCH, None), P(DP, BATCH), P(DP, BATCH), P())
    out_specs = (P(DP, BATCH, None), P(DP, BATCH, None), P((*BATCH, *DP), None))
    return jax.shard_map(body, mesh=fine, in_specs=in_specs, out_specs=out_specs, check_vma=False)
```

```python
import jax
import jax.numpy as jnp
from jax import lax
from jax.experimental import pallas as pl
from jax.experimental.pallas import tpu as pltpu
from jax.sharding import Mesh, PartitionSpec as P

ROWS = 128
AXES = ("z", "xh", "y", "xl", "c")
SIZES = (16, 2, 4, 2, 2)
BATCH = ("z", "xh", "y")
PLANE = ("xh", "xl", "y")
DP = ("xl", "c")
WIDTH = 1024
HALF = WIDTH // 2

VMEM = pl.BlockSpec(memory_space=pltpu.VMEM)
HBM = pl.BlockSpec(memory_space=pltpu.HBM)

score_scale = 0.1
bf16 = jnp.bfloat16
f32 = jnp.float32


def shifted(block, distance):
    n = lax.axis_size(BATCH)
    return lax.ppermute(block, BATCH, [(i, (i + distance) % n) for i in range(n)])


def mm(a, b):
    return jnp.dot(a, b, preferred_element_type=f32)


def nt(a, b):
    return lax.dot_general(a, b, (((1,), (1,)), ((), ())), preferred_element_type=f32)


def make_pick(core, pick_ref):
    pos = lax.broadcasted_iota(jnp.int32, (WIDTH, 128), 0)
    lane = lax.broadcasted_iota(jnp.int32, (WIDTH, 128), 1)
    plane, z, t = (pos >> 5) & 15, (pos >> 1) & 15, pos & 1
    c = jnp.where(pos < HALF, 1 - core, core)
    row = z * 64 + (plane >> 3) * 32 + (plane & 3) * 8 + ((plane >> 2) & 1) * 4 + c * 2 + t
    for j in range(WIDTH // 128):
        pick_ref[:, j * 128 : (j + 1) * 128] = jnp.where(row == lane + j * 128, 1.0, 0.0).astype(bf16)


def upright(row):
    return jnp.broadcast_to(row, (ROWS, ROWS)).T[:, :1]


def grads_kernel(
    core_ref, weight_ref, positive_ref, hq_any, hp_any, hp1_any, hp2_any, w_any,
    note_any, gq_any, theirs_any, own_any, g_any,
    states_ref, e_ref, pick_ref, held_ref, g_ref, note_keep, w_ref, theirs_ref, sems,
):
    into = [
        pltpu.make_async_copy(block, states_ref.at[i * ROWS : (i + 1) * ROWS], sems.at[i])
        for i, block in enumerate((hq_any, hp_any, hp1_any, hp2_any))
    ]
    into.append(pltpu.make_async_copy(w_any, w_ref, sems.at[6]))
    for copy in into:
        copy.start()
    weight = upright(weight_ref[...])
    local = upright((positive_ref[...] & (ROWS - 1)).astype(f32)).astype(jnp.int32)
    make_pick(core_ref[0], pick_ref)
    for copy in into:
        copy.wait()
    e_ref[...] = mm(states_ref[...], w_ref[...]).astype(bf16)
    scores = nt(e_ref[:ROWS], e_ref[ROWS:]) * score_scale
    held_ref[...] = nt(pick_ref[...], states_ref[...]).astype(bf16)
    top = jnp.max(scores, axis=1, keepdims=True)
    lse = top + jnp.log(jnp.sum(jnp.exp(scores - top), axis=1, keepdims=True))
    column = lax.broadcasted_iota(jnp.int32, (ROWS, 3 * ROWS), 1)
    onehot = jnp.where(column == local, 1.0, 0.0)
    ds = (weight * score_scale * (jnp.exp(scores - lse) - onehot)).astype(bf16)
    which = lax.broadcasted_iota(jnp.int32, (ROWS, ROWS), 1)
    note = jnp.where(which == 0, lse, jnp.where(which == 1, weight * score_scale, 0.0))
    note_keep[...] = note.T[:8]
    g_ref[:ROWS] = mm(ds, e_ref[ROWS:]).astype(bf16)
    g_ref[ROWS:] = mm(ds.astype(f32).T.astype(bf16), e_ref[:ROWS]).astype(bf16)
    out = [
        pltpu.make_async_copy(note_keep, note_any, sems.at[4]),
        pltpu.make_async_copy(g_ref.at[:ROWS], gq_any, sems.at[5]),
        pltpu.make_async_copy(held_ref.at[HALF:], own_any, sems.at[7]),
        pltpu.make_async_copy(g_ref, g_any, sems.at[8]),
    ]
    for copy in out:
        copy.start()
    for i in range(2):
        rows = slice(i * HALF // 2, (i + 1) * HALF // 2)
        theirs_ref[rows] = mm(held_ref[rows], g_ref[...]).astype(bf16)
        out.append(pltpu.make_async_copy(theirs_ref.at[rows], theirs_any.at[rows], sems.at[9 + i]))
        out[-1].start()
    for copy in out:
        copy.wait()


def own_kernel(held_ref, g_ref, mine_ref):
    mine_ref[...] = mm(held_ref[...], g_ref[...])


def query_kernel(gq_ref, w_ref, out_ref):
    out_ref[...] = nt(gq_ref[...], w_ref[...]).astype(bf16)


def later_kernel(hq_ref, hq1_ref, hq2_ref, w_ref, hp_ref, eq_ref, scores_ref, all_ref):
    all_ref[:ROWS] = hq_ref[...]
    all_ref[ROWS : 2 * ROWS] = hq1_ref[...]
    all_ref[2 * ROWS :] = hq2_ref[...]
    eq_ref[...] = mm(all_ref[...], w_ref[...]).astype(bf16)
    ep = mm(hp_ref[...], w_ref[...]).astype(bf16)
    scores_ref[...] = nt(ep, eq_ref[...]) * score_scale


def passage_kernel(positive_ref, eq_ref, scores_ref, note0_ref, note1_ref, note2_ref, w_ref, out_ref):
    passage = lax.broadcasted_iota(jnp.int32, (ROWS, ROWS), 0)
    onehot = jnp.where(passage == (positive_ref[...] & (ROWS - 1)), 1.0, 0.0)
    gep = jnp.zeros((ROWS, WIDTH), f32)
    for k, note_ref in enumerate((note0_ref, note1_ref, note2_ref)):
        own = slice(k * ROWS, (k + 1) * ROWS)
        p = jnp.exp(scores_ref[:, own] - note_ref[0:1, :])
        ds = note_ref[1:2, :] * (p - onehot if k == 0 else p)
        gep = gep + mm(ds.astype(bf16), eq_ref[own])
    out_ref[...] = nt(gep.astype(bf16), w_ref[...]).astype(bf16)


def join_kernel(mine_ref, swapped_ref, out_ref, sum_ref, sems):
    copies = []
    for i in range(4):
        rows = slice(i * ROWS, (i + 1) * ROWS)
        sum_ref[rows] = (mine_ref[rows] + swapped_ref[rows].astype(f32)).astype(bf16)
        copies.append(pltpu.make_async_copy(sum_ref.at[rows], out_ref.at[rows], sems.at[i]))
        copies[i].start()
    for copy in copies:
        copy.wait()


def plane_kernel(pieces_ref, out_ref):
    total = pieces_ref[0].astype(f32)
    for i in range(1, 16):
        total = total + pieces_ref[i].astype(f32)
    for k in range(8):
        out_ref[:, k, :] = total[:, k * 128 : (k + 1) * 128]


def shape(rows, columns, dtype):
    return jax.ShapeDtypeStruct((rows, columns), dtype)


def call(kernel, outs, *args, scratch=(), smem=0, anywhere=0, weighs=1, out_specs=None, limit=16):
    if out_specs is None:
        out_specs = jax.tree.map(lambda _: VMEM, outs)
    vmem = len(args) - smem - anywhere
    return pl.pallas_call(
        kernel,
        out_shape=outs,
        in_specs=[pl.BlockSpec(memory_space=pltpu.SMEM)] * smem
        + [VMEM] * vmem
        + [HBM] * anywhere,
        out_specs=out_specs,
        scratch_shapes=list(scratch),
        compiler_params=pltpu.CompilerParams(vmem_limit_bytes=limit * 2**20),
        cost_estimate=pl.CostEstimate(
            flops=weighs * 2 * ROWS * WIDTH * WIDTH, bytes_accessed=2**20, transcendentals=0
        ),
    )(*args)


def body(query_states, passage_states, loss_weights, positives, head_weight):
    hq = query_states[0]
    hp = passage_states[0]
    square = shape(ROWS, WIDTH, bf16)

    hp1 = shifted(hp, 1)
    hp2 = shifted(hp, 2)
    hq2 = shifted(hq, -2)
    hq1 = shifted(hq, -1)

    core = lax.axis_index("c").astype(jnp.int32).reshape(1)
    half = shape(HALF, WIDTH, bf16)
    note, gq, theirs, own, grads = call(
        grads_kernel,
        (shape(8, ROWS, f32), square, half, shape(HALF, 4 * ROWS, bf16), shape(4 * ROWS, WIDTH, bf16)),
        core, loss_weights, positives, hq, hp, hp1, hp2, head_weight,
        smem=1, anywhere=5, out_specs=(HBM,) * 5, limit=56,
        scratch=[
            pltpu.VMEM((4 * ROWS, WIDTH), bf16),
            pltpu.VMEM((4 * ROWS, WIDTH), bf16),
            pltpu.VMEM((WIDTH, WIDTH), bf16),
            pltpu.VMEM((WIDTH, 4 * ROWS), bf16),
            pltpu.VMEM((4 * ROWS, WIDTH), bf16),
            pltpu.VMEM((8, ROWS), f32),
            pltpu.VMEM((WIDTH, WIDTH), bf16),
            pltpu.VMEM((HALF, WIDTH), bf16),
            pltpu.SemaphoreType.DMA((11,)),
        ],
    )
    theirs, hq1, hq2 = lax.optimization_barrier((theirs, hq1, hq2))
    swapped = lax.ppermute(theirs, "c", [(0, 1), (1, 0)])
    mine = call(own_kernel, shape(HALF, WIDTH, f32), own, grads)
    chip = call(
        join_kernel, shape(HALF, WIDTH, bf16), mine, swapped, out_specs=HBM,
        scratch=[pltpu.VMEM((HALF, WIDTH), bf16), pltpu.SemaphoreType.DMA((4,))],
    )
    chip, gq = lax.optimization_barrier((chip, gq))
    pieces = lax.all_to_all(chip, PLANE, 0, 0, tiled=True)
    plane = call(
        plane_kernel, jax.ShapeDtypeStruct((32, 8, 128), f32), pieces.reshape(16, 32, WIDTH)
    )
    plane, note = lax.optimization_barrier((plane, note))
    pieces = lax.all_to_all(plane.reshape(16, 16, 128), "z", 0, 0, tiled=True)
    note1 = shifted(note, -1)
    note2 = shifted(note, -2)
    eq3, scores = call(
        later_kernel,
        (shape(3 * ROWS, WIDTH, bf16), shape(ROWS, 3 * ROWS, f32)),
        hq, hq1, hq2, head_weight, hp,
        scratch=[pltpu.VMEM((3 * ROWS, WIDTH), bf16)],
    )
    grad_q = call(query_kernel, square, gq, head_weight)
    grad_p = call(passage_kernel, square, positives, eq3, scores, note, note1, note2, head_weight)
    head_grad = jnp.sum(pieces.reshape(16, 16, 128), axis=0).reshape(2, 1024)
    return (grad_q[None], grad_p[None], head_grad)


def solution(mesh):
    fine = Mesh(mesh.devices.reshape(SIZES), AXES)
    in_specs = (P(DP, BATCH, None), P(DP, BATCH, None), P(DP, BATCH), P(DP, BATCH), P())
    out_specs = (P(DP, BATCH, None), P(DP, BATCH, None), P((*BATCH, *DP), None))
    return jax.shard_map(body, mesh=fine, in_specs=in_specs, out_specs=out_specs, check_vma=False)
```
